128 devices in a mesh: node: 16 (over y, z), chan: 8 (over x, core).
Axes of the slice: x: 4, y: 4, z: 4, core: 2. Of those that a mesh axis runs over, the one named last changes fastest.
Arguments:
- latents: bfloat16 [12288, 1024], P('node', 'chan'), may hold values from -6 to 6
- edge_attr: bfloat16 [24576, 1024], P('node', 'chan'), may hold values from -6 to 6
- edge_src: int32 [24576], P('node'), may hold values from 0 to 4863, as said below
- edge_dst: int32 [24576], P('node'), may hold values from 0 to 767
- send_blocks: int32 [16, 16, 2], P('node'), may hold values from 0 to 5
- edge_hidden_w: bfloat16 [3072, 1024], P(None, 'chan'), may hold values from -0.109375 to 0.109375
- edge_out_w: bfloat16 [1024, 1024], P('chan'), may hold values from -0.1875 to 0.1875
- node_hidden_w: bfloat16 [2048, 1024], P(None, 'chan'), may hold values from -0.125 to 0.125
- node_out_w: bfloat16 [1024, 1024], P('chan'), may hold values from -0.1875 to 0.1875
- node_cotangent: bfloat16 [12288, 1024], P('node', 'chan'), may hold values from -6 to 6
- edge_cotangent: bfloat16 [24576, 1024], P('node', 'chan'), may hold values from -6 to 6
Outputs:
- grad_latents: float32 [12288, 1024], P('node', 'chan')
- grad_edges: float32 [24576, 1024], P('node', 'chan')
- grad_edge_hidden: float32 [3072, 1024], P('node', 'chan')
- grad_edge_out: float32 [1024, 1024], P('chan', 'node')
- grad_node_hidden: float32 [2048, 1024], P('node', 'chan')
- grad_node_out: float32 [1024, 1024], P('chan', 'node')
The draws below stay inside these ranges and needn't reach their ends.
Inputs may be any that keep to these rules, and one draw needn't show every extreme that they name: `edge_src`: On each node device half of the edges have a source among its own nodes and half in its halo table, and every halo slot (p, s) is the source of exactly 24 of its edges. send_blocks[p, q, s] is the block of node device p that device q holds as halo slot s.
All inputs are finite; a program needn't handle non-finite values.
Results may differ from the reference program's by a relative error of at most 0.025.
Values may be sent and summed in bfloat16 or wider, within the bound.
A program may use at most 192 MiB of HBM per device.

```python
import jax
import jax.numpy as jnp
from jax import lax

LATENT = 1024
BLOCK = 128
NODE_BLOCKS = 6
HALO_BLOCKS = 2
EDGES_DEV = 1536
NODES_DEV = 768
NODES = 12288
EDGES = 24576
HALO_ROWS = 4096
N_NODE = 16
N_CHAN = 8


def draw_edge_src(key, part):
    key = jax.random.fold_in(key, 11)
    key_local, key_row, key_order = jax.random.split(key, 3)
    devices = EDGES // EDGES_DEV
    half = EDGES_DEV // 2
    slots = HALO_ROWS // BLOCK
    local_rows = jax.random.randint(key_local, (devices, half), 0, NODES_DEV, dtype=jnp.int32)
    local_rows = local_rows.at[:, 0].set(0)
    slot_ids = (jnp.arange(half, dtype=jnp.int32) % slots)[None, :]
    block_rows = jax.random.randint(key_row, (devices, half), 0, BLOCK, dtype=jnp.int32)
    far_rows = NODES_DEV + slot_ids * BLOCK + block_rows
    far_rows = far_rows.at[:, half - 1].set(NODES_DEV + HALO_ROWS - 1)
    joined = jnp.concatenate([local_rows, far_rows], axis=1)
    shuffled = jax.random.permutation(key_order, joined, axis=1, independent=True)
    return shuffled.reshape(EDGES).astype(jnp.int32)


def place_ends(result, own_key, smallest, high):
    dims = result.shape
    spot = [jax.random.randint(jax.random.fold_in(own_key, axis), (), 0, dims[axis]) for axis in range(len(dims))]
    result = result.at[tuple(spot)].set(smallest)
    longest = dims.index(max(dims))
    spot[longest] = (spot[longest] + 1) % dims[longest]
    return result.at[tuple(spot)].set(high)


def with_spikes(array, own_key, source, target, shards_of, factor):
    owner, partner = [(jnp.arange(array.shape[axis_at]) // (array.shape[axis_at] // shards_of)).reshape([-1 if axis == axis_at else 1 for axis in range(array.ndim)]) for axis_at in (source, target)]
    chosen = jax.random.permutation(own_key, shards_of)[partner]
    strong = (owner == chosen) | (owner == (partner + shards_of // 2) % shards_of)
    return jnp.where(strong, factor * array, array)


def shard_levels(rng, dims, cuts, smallest, largest):
    gain, own = 1.0, jax.random.fold_in(rng, 6)
    for dim, parts in cuts:
        draws = jnp.exp(jax.random.uniform(jax.random.fold_in(own, dim), (parts,), jnp.float32, smallest / len(cuts), largest / len(cuts)))
        gain = gain * jnp.repeat(draws, dims[dim] // parts).reshape([-1 if axis == dim else 1 for axis in range(len(dims))])
    return gain


def noise(own_key, dims, scale, reach, cuts=(), kind=jnp.bfloat16):
    drawn = jax.random.normal(own_key, dims, jnp.float32) * scale
    if len(cuts) > 0:
        drawn = shard_levels(own_key, dims, cuts, -0.22, 0.18) * drawn
    return jnp.clip(drawn, min=-reach, max=reach).astype(kind)


def gaussian_with(stream_key, extent, scale, most, shards, heavy, held_as=jnp.bfloat16):
    entries = scale * jax.random.normal(stream_key, extent, jnp.float32)
    if shards:
        entries = entries * shard_levels(stream_key, extent, shards, -0.22, 0.18)
    return jnp.clip(with_spikes(entries, jax.random.fold_in(stream_key, 3), *heavy), -most, most).astype(held_as)


def setup_inputs(seed: int = 0) -> dict:
    seeds = jax.random.split(jax.random.key(seed), 12)
    return {
        "latents": noise(seeds[0], (NODES, LATENT), 1.0, 6.0, ((0, 16), (1, 8))),
        "edge_attr": noise(seeds[1], (EDGES, LATENT), 1.0, 6.0, ((0, 16), (1, 8))),
        "edge_src": draw_edge_src(jax.random.fold_in(seeds[11], 71), 0),
        "edge_dst": place_ends(jax.random.randint(seeds[3], (EDGES,), 0, NODES_DEV), jax.random.fold_in(seeds[3], 1), 0, NODES_DEV - 1).astype(jnp.int32),
        "send_blocks": place_ends(jax.random.randint(seeds[4], (N_NODE, N_NODE, HALO_BLOCKS), 0, NODE_BLOCKS), jax.random.fold_in(seeds[4], 1), 0, NODE_BLOCKS - 1).astype(jnp.int32),
        "edge_hidden_w": noise(seeds[5], (3 * LATENT, LATENT), (3 * LATENT) ** -0.5, 0.109375, ((1, 8),)),
        "edge_out_w": noise(seeds[6], (LATENT, LATENT), LATENT ** -0.5, 0.1875, ((0, 8),)),
        "node_hidden_w": noise(seeds[7], (2 * LATENT, LATENT), (2 * LATENT) ** -0.5, 0.125, ((1, 8),)),
        "node_out_w": noise(seeds[8], (LATENT, LATENT), LATENT ** -0.5, 0.1875, ((0, 8),)),
        "node_cotangent": gaussian_with(seeds[9], (NODES, LATENT), 1.0, 6.0, ((0, 16), (1, 8)), (0, 1, 16, 2.0)),
        "edge_cotangent": gaussian_with(seeds[10], (EDGES, LATENT), 1.0, 6.0, ((0, 16), (1, 8)), (0, 1, 16, 2.0)),
    }


def silu_grad(value):
    sig = jax.nn.sigmoid(value)
    return sig * (1.0 + value * (1.0 - sig))

def split_product(left, right):
    width = left.shape[1] // N_CHAN
    total = jnp.zeros((left.shape[0], right.shape[1]), jnp.float32)
    for group in range(N_CHAN):
        piece = jnp.dot(left[:, group * width:(group + 1) * width], right[group * width:(group + 1) * width], preferred_element_type=jnp.float32)
        rounded = lax.optimization_barrier(piece.astype(jnp.bfloat16))
        total = total + rounded.astype(jnp.float32)
    return total

def reference(latents, edge_attr, edge_src, edge_dst, send_blocks, edge_hidden_w, edge_out_w, node_hidden_w, node_out_w, node_cotangent, edge_cotangent):
    edge_scale = float(EDGES) ** (-0.5)
    node_scale = float(NODES) ** (-0.5)
    halo_range = jnp.arange(HALO_ROWS, dtype=jnp.int32)

    def device_step(carry, device):
        grad_nodes, acc_eh, acc_eo, acc_nh, acc_no = carry
        node_start = (device * NODES_DEV).astype(jnp.int32)
        edge_start = (device * EDGES_DEV).astype(jnp.int32)
        own_latents = lax.dynamic_slice_in_dim(latents, node_start, NODES_DEV, 0)
        own_edges = lax.dynamic_slice_in_dim(edge_attr, edge_start, EDGES_DEV, 0)
        sources = lax.dynamic_slice_in_dim(edge_src, edge_start, EDGES_DEV, 0)
        targets = lax.dynamic_slice_in_dim(edge_dst, edge_start, EDGES_DEV, 0)
        node_cot = lax.dynamic_slice_in_dim(node_cotangent, node_start, NODES_DEV, 0)
        edge_cot = lax.dynamic_slice_in_dim(edge_cotangent, edge_start, EDGES_DEV, 0)
        is_local = sources < NODES_DEV
        far_rows = jnp.maximum(sources - NODES_DEV, 0).astype(jnp.int32)
        owner = far_rows // (HALO_BLOCKS * BLOCK)
        which = far_rows // BLOCK % HALO_BLOCKS
        chosen = send_blocks[owner, device, which]
        source_index = jnp.where(is_local, node_start + sources, owner * NODES_DEV + chosen * BLOCK + far_rows % BLOCK).astype(jnp.int32)
        edge_inputs = jnp.concatenate([latents[source_index], own_latents[targets], own_edges], axis=1)
        hidden_pre = jnp.dot(edge_inputs, edge_hidden_w, preferred_element_type=jnp.float32)
        hidden = jax.nn.silu(hidden_pre).astype(jnp.bfloat16)
        messages = split_product(hidden, edge_out_w)
        new_edges = (own_edges.astype(jnp.float32) + messages).astype(jnp.bfloat16)
        node_sum = jax.ops.segment_sum(new_edges.astype(jnp.float32), targets, num_segments=NODES_DEV).astype(jnp.bfloat16)
        node_inputs = jnp.concatenate([own_latents, node_sum], axis=1)
        node_pre = jnp.dot(node_inputs, node_hidden_w, preferred_element_type=jnp.float32)
        node_hidden = jax.nn.silu(node_pre).astype(jnp.bfloat16)
        acc_no = acc_no + node_scale * jnp.dot(node_hidden.T, node_cot, preferred_element_type=jnp.float32)
        node_hidden_grad = (jnp.dot(node_cot, node_out_w.T, preferred_element_type=jnp.float32) * silu_grad(node_pre)).astype(jnp.bfloat16)
        acc_nh = acc_nh + node_scale * jnp.dot(node_inputs.T, node_hidden_grad, preferred_element_type=jnp.float32)
        node_input_grad = split_product(node_hidden_grad, node_hidden_w.T)
        edge_total = edge_cot.astype(jnp.float32) + node_input_grad[:, LATENT:][targets]
        message_grad = edge_total.astype(jnp.bfloat16)
        acc_eo = acc_eo + edge_scale * jnp.dot(hidden.T, message_grad, preferred_element_type=jnp.float32)
        edge_hidden_grad = (jnp.dot(message_grad, edge_out_w.T, preferred_element_type=jnp.float32) * silu_grad(hidden_pre)).astype(jnp.bfloat16)
        acc_eh = acc_eh + edge_scale * jnp.dot(edge_inputs.T, edge_hidden_grad, preferred_element_type=jnp.float32)
        edge_input_grad = split_product(edge_hidden_grad, edge_hidden_w.T)
        grad_edge_rows = edge_total + edge_input_grad[:, 2 * LATENT:]
        source_grad = edge_input_grad[:, :LATENT]
        local_grad = jnp.where(is_local[:, None], source_grad, 0.0)
        far_grad = jnp.where(is_local[:, None], 0.0, source_grad)
        own_grad = node_cot.astype(jnp.float32) + node_input_grad[:, :LATENT]
        own_grad = own_grad + jax.ops.segment_sum(edge_input_grad[:, LATENT:2 * LATENT], targets, num_segments=NODES_DEV)
        own_grad = own_grad + jax.ops.segment_sum(local_grad, jnp.where(is_local, sources, 0).astype(jnp.int32), num_segments=NODES_DEV)
        halo_sum = jax.ops.segment_sum(far_grad, far_rows, num_segments=HALO_ROWS)
        halo_grad = lax.optimization_barrier(halo_sum.astype(jnp.bfloat16)).astype(jnp.float32)
        halo_owner = halo_range // (HALO_BLOCKS * BLOCK)
        halo_which = halo_range // BLOCK % HALO_BLOCKS
        halo_index = (halo_owner * NODES_DEV + send_blocks[halo_owner, device, halo_which] * BLOCK + halo_range % BLOCK).astype(jnp.int32)
        grad_nodes = grad_nodes.at[halo_index].add(halo_grad)
        grad_nodes = grad_nodes.at[node_start + jnp.arange(NODES_DEV, dtype=jnp.int32)].add(own_grad)
        return ((grad_nodes, acc_eh, acc_eo, acc_nh, acc_no), grad_edge_rows)
    start = (jnp.zeros((NODES, LATENT), jnp.float32), jnp.zeros((3 * LATENT, LATENT), jnp.float32), jnp.zeros((LATENT, LATENT), jnp.float32), jnp.zeros((2 * LATENT, LATENT), jnp.float32), jnp.zeros((LATENT, LATENT), jnp.float32))
    final, edge_rows = lax.scan(device_step, start, jnp.arange(N_NODE, dtype=jnp.int32))
    grad_nodes, acc_eh, acc_eo, acc_nh, acc_no = final
    return (grad_nodes, edge_rows.reshape(EDGES, LATENT), acc_eh, acc_eo, acc_nh, acc_no)
```

```python
import functools

import jax
import jax.numpy as jnp
from jax import lax
from jax.experimental import pallas as pl
from jax.experimental.pallas import tpu as pltpu
from jax.sharding import PartitionSpec as P

BF = jnp.bfloat16
F32 = jnp.float32
LANE = 128
NC = 2


def mm(a, b):
    return jnp.dot(a, b, preferred_element_type=F32)


def mm_nt(a, b):
    return lax.dot_general(a, b, (((1,), (1,)), ((), ())), preferred_element_type=F32)


def mm_tn(a, b):
    return lax.dot_general(a, b, (((0,), (0,)), ((), ())), preferred_element_type=F32)


def one_hot(mask):
    return jnp.where(mask, 1.0, 0.0).astype(BF)


def lane_iota(rows):
    return lax.broadcasted_iota(jnp.int32, (rows, LANE), 1).astype(F32)


def sublane_iota(rows):
    return lax.broadcasted_iota(jnp.int32, (rows, LANE), 0).astype(F32)


def select_lanes(index, width):
    lanes = lane_iota(index.shape[0])
    return jnp.concatenate(
        [one_hot(index == lanes + float(b * LANE)) for b in range(width // LANE)], axis=1
    )


def wide(ref, lead=()):
    groups = ref.shape[len(lead)]
    return jnp.concatenate([ref[(*lead, g)] for g in range(groups)], axis=1)


def kernel(
    dims,
    lat, ea, src, dst, sb, weh, weo, wnh, wno, nct, ect,
    gl, ge, out_eh, out_eo, out_nh, out_no,
    ssem, rsem,
    ei, ni, cot, mg, hidden, hpre, npre,
    src_b, dst_b, q_b, dt, slt, pt, rsel,
    rq_out, rq_in, row_out, row_in, ret_out, ret_in,
    srcc, dstc, nsum, mgc,
    w_eh, w_nh, w_no, w_eo,
    g_eh, g_nh, g_no, g_eo,
    pb_m, rx_m, ch_m, pb_n, rx_n, ch_n, pb_e, rx_e, ch_e,
    *rs_bufs,
):
    NX, NY, NZ = dims
    NN = NY * NZ
    E, N = ea.shape[0], lat.shape[0]
    RE, RN = E // NX, N // NX
    L = NX * NC * LANE
    HC = NX * LANE
    PER = E // 2 // NN
    SLOT = PER // 2
    edge_scale = float(E * NN) ** (-0.5)
    node_scale = float(N * NN) ** (-0.5)

    n, k = lax.axis_index("node"), lax.axis_index("chan")
    x, c = k // NC, k % NC
    y, z = n // NZ, n % NZ

    def at_x(j):
        return (x + j) % NX

    def x_peer(j):
        return (n, at_x(j) * NC + c)

    def y_peer(j):
        return (((y + j) % NY) * NZ + z, k)

    def z_peer(j):
        return (y * NZ + (z + j) % NZ, k)

    def n_peer(j):
        return ((n + j) % NN, k)

    sib = (n, x * NC + 1 - c)

    pending = []
    used = [0]

    def rcopy(a, b, device):
        i = used[0]
        used[0] += 1
        copy = pltpu.make_async_remote_copy(
            src_ref=a, dst_ref=b, send_sem=ssem.at[i], recv_sem=rsem.at[i],
            device_id=device, device_id_type=pl.DeviceIdType.MESH,
        )
        copy.start()
        pending.append(copy)
        return copy

    def flush():
        while pending:
            pending.pop(0).wait_send()

    far_first = sorted(range(1, NX), key=lambda j: -min(j, NX - j))

    class ToRows:
        def __init__(self, put):
            self.put, self.near, self.far = put, [], []

        def send(self, j, chunk):
            if j:
                self.far.append((j, rcopy(chunk, self.put(x * NC + c), x_peer(j))))
            else:
                self.put(x * NC + c)[...] = chunk[...]
                self.near.append(rcopy(chunk, self.put(x * NC + c), sib))
            return self

        def send_all(self, chunk):
            for j in [*far_first, 0]:
                self.send(j, chunk(at_x(j)))
            return self

        def forward(self):
            for j, copy in self.far:
                copy.wait_recv()
                slot = self.put(at_x(NX - j) * NC + c)
                self.near.append(rcopy(slot, slot, sib))

        def wait(self):
            for copy in self.near:
                copy.wait_recv()

    class ToChan:
        def __init__(self, value, pb, rx, ch):
            self.pb, self.rx, self.ch, self.far = pb, rx, ch, []
            for g in range(NX * NC):
                pb[g // NC, g % NC] = value[:, g * LANE:(g + 1) * LANE].astype(BF)
            self.near = [
                (j, rcopy(pb.at[at_x(j), 1 - c], rx.at[at_x(j)], sib)) for j in [*far_first, 0]
            ]

        def forward(self):
            for j, copy in self.near:
                copy.wait_recv()
                xx = at_x(j)
                total = (self.rx[xx].astype(F32) + self.pb[xx, c].astype(F32)).astype(BF)
                if j:
                    self.rx[xx] = total
                    self.far.append(rcopy(self.rx.at[xx], self.ch.at[x], x_peer(j)))
                else:
                    self.ch[x] = total

        def wait(self):
            for copy in self.far:
                copy.wait_recv()

    class Gather:
        def __init__(self, w):
            self.w, self.half = w, w.shape[2] // 2

        def step1(self, own):
            w = self.w
            self.copies = [
                rcopy(own, w.at[y, z, :, pl.ds((NX - j) * LANE, LANE)], x_peer(j))
                for j in range(1, NX)
            ]

        def _recv(self):
            for copy in self.copies:
                copy.wait_recv()

        def step2(self):
            self._recv()
            w, h = self.w, self.half
            a = w.at[y, z, pl.ds(0, h), pl.ds(LANE, HC - LANE)]
            b = w.at[y, z, pl.ds(h, h), pl.ds(LANE, HC - LANE)]
            self.copies = [rcopy(a, a, z_peer(j)) for j in range(1, NZ)]
            self.copies += [rcopy(b, b, y_peer(j)) for j in range(1, NY)]

        def step3(self):
            self._recv()
            w, h = self.w, self.half
            a = w.at[y, :, pl.ds(0, h), pl.ds(LANE, HC - LANE)]
            b = w.at[:, z, pl.ds(h, h), pl.ds(LANE, HC - LANE)]
            self.copies = [rcopy(a, a, y_peer(j)) for j in range(1, NY)]
            self.copies += [rcopy(b, b, z_peer(j)) for j in range(1, NZ)]

        def wait(self):
            self._recv()

    class Scatter:
        def __init__(self, g, bufs):
            self.g = g
            self.ra, self.rb, self.sa, self.sbb, self.ra2, self.rb2, self.s2, self.r3 = bufs

        def step1(self):
            g, half = self.g, HC // 2
            self.a = [
                rcopy(g.at[:, (z + j) % NZ, :, pl.ds(0, half)], self.ra.at[j - 1], z_peer(j))
                for j in range(1, NZ)
            ]
            self.b = [
                rcopy(g.at[(y + j) % NY, :, :, pl.ds(half, half)], self.rb.at[j - 1], y_peer(j))
                for j in range(1, NY)
            ]

        def step2(self):
            g, half = self.g, HC // 2
            for copy in self.a:
                copy.wait_recv()
            for yy in range(NY):
                total = g[yy, z, :, 0:half].astype(F32)
                for j in range(1, NZ):
                    total = total + self.ra[j - 1, yy].astype(F32)
                self.sa[yy] = total.astype(BF)
            self.a = [
                rcopy(self.sa.at[(y + j) % NY], self.ra2.at[j - 1], y_peer(j))
                for j in range(1, NY)
            ]
            for copy in self.b:
                copy.wait_recv()
            for zz in range(NZ):
                total = g[y, zz, :, half:HC].astype(F32)
                for j in range(1, NY):
                    total = total + self.rb[j - 1, zz].astype(F32)
                self.sbb[zz] = total.astype(BF)
            self.b = [
                rcopy(self.sbb.at[(z + j) % NZ], self.rb2.at[j - 1], z_peer(j))
                for j in range(1, NZ)
            ]

        def step3(self):
            half = HC // 2
            for copy in self.a:
                copy.wait_recv()
            total = self.sa[y].astype(F32)
            for j in range(1, NY):
                total = total + self.ra2[j - 1].astype(F32)
            self.s2[:, 0:half] = total.astype(BF)
            for copy in self.b:
                copy.wait_recv()
            total = self.sbb[z].astype(F32)
            for j in range(1, NZ):
                total = total + self.rb2[j - 1].astype(F32)
            self.s2[:, half:HC] = total.astype(BF)
            self.x = [
                rcopy(self.s2.at[:, pl.ds(j * LANE, LANE)], self.r3.at[j - 1], x_peer(j))
                for j in range(1, NX)
            ]

        def finish(self):
            for copy in self.x:
                copy.wait_recv()
            total = self.s2[:, 0:LANE].astype(F32)
            for j in range(1, NX):
                total = total + self.r3[j - 1].astype(F32)
            return total

    barrier = pltpu.get_barrier_semaphore()
    partners = [x_peer(j) for j in range(1, NX)] + [sib] + [n_peer(j) for j in range(1, NN)]
    for device in partners:
        pl.semaphore_signal(barrier, inc=1, device_id=device, device_id_type=pl.DeviceIdType.MESH)
    pl.semaphore_wait(barrier, len(partners))

    ch_eh, ch_nh = weh.shape[0] // NN, wnh.shape[0] // NN
    gat_eh, gat_nh, gat_no, gat_eo = Gather(w_eh), Gather(w_nh), Gather(w_no), Gather(w_eo)
    gat_eh.step1(weh.at[pl.ds(n * ch_eh, ch_eh), :])
    rows_ea = ToRows(lambda g: ei.at[2, g]).send_all(lambda xx: ea.at[pl.ds(xx * RE, RE), :])

    srcf = src[...].astype(F32)
    dstf = dst[...].astype(F32)
    is_far = srcf >= float(N)
    slotf = jnp.where(is_far, jnp.floor((srcf - float(N)) * (1.0 / LANE)), -1.0)
    blocks = E // LANE
    for b in range(blocks):
        piece = slice(b * LANE, (b + 1) * LANE)
        src_b[piece, :] = jnp.broadcast_to(srcf[:, piece], (LANE, LANE)).T
        dst_b[piece, :] = jnp.broadcast_to(dstf[:, piece], (LANE, LANE)).T
    src_col = src_b[...]
    slot_col = jnp.where(
        src_col >= float(N), jnp.floor((src_col - float(N)) * (1.0 / LANE)), -1.0
    )
    order = sublane_iota(E)
    place = sublane_iota(NN * PER)
    for b in range(blocks):
        piece = slice(b * LANE, (b + 1) * LANE)
        mine = jnp.broadcast_to(slotf[:, piece], (E, LANE))
        before = (slot_col == mine) & (order < lane_iota(E) + float(b * LANE))
        rank = jnp.sum(jnp.where(before, 1.0, 0.0), axis=0, keepdims=True)
        q = jnp.where(is_far[:, piece], slotf[:, piece] * float(SLOT) + rank, -1.0)
        pt[:, piece] = one_hot(place == jnp.broadcast_to(q, (NN * PER, LANE)))
        q_b[piece, :] = jnp.broadcast_to(q, (LANE, LANE)).T
    row_in_block = (src_col - LANE * jnp.floor(src_col * (1.0 / LANE))).astype(BF)
    wanted = mm(pt[...], row_in_block).astype(BF)
    for p in range(NN):
        rq_out[p] = wanted[p * PER:(p + 1) * PER]
    ask = [
        rcopy(rq_out.at[(n + j) % NN], rq_in.at[n], n_peer(j)) for j in range(1, NN)
    ]
    rq_in[n] = rq_out[n]

    rows_dst = ToRows(lambda g: ei.at[1, g])
    for j in [*far_first, 0]:
        xx = at_x(j)
        pick = select_lanes(dst_b[pl.ds(xx * RE, RE), :], N)
        dstc[xx] = mm(pick, lat[...]).astype(BF)
        rows_dst.send(j, dstc.at[xx])

    gat_eh.step2()

    w_eh[:, :, :, 0:LANE] = weh[...].reshape(NY, NZ, ch_eh, LANE)
    w_nh[:, :, :, 0:LANE] = wnh[...].reshape(NY, NZ, ch_nh, LANE)
    w_eo[:, :, :, 0:LANE] = weo[...].T.reshape(NY, NZ, L // NN, LANE)
    w_no[:, :, :, 0:LANE] = wno[...].T.reshape(NY, NZ, L // NN, LANE)
    for gather in (gat_eo, gat_nh, gat_no):
        gather.step1(gather.w.at[y, z, :, pl.ds(0, LANE)])

    for copy in ask:
        copy.wait_recv()
    half_rows = sublane_iota(PER) < float(SLOT)
    for d in range(NN):
        base = jnp.where(
            half_rows,
            (sb[0, d, 0] * LANE).astype(F32),
            (sb[0, d, 1] * LANE).astype(F32),
        )
        rsel[d] = select_lanes(rq_in[d].astype(F32) + base, N)
    given = mm(rsel[...].reshape(NN * PER, N), lat[...]).astype(BF)
    for d in range(NN):
        row_out[d] = given[d * PER:(d + 1) * PER]
    halo = [
        rcopy(row_out.at[(n + j) % NN], row_in.at[n], n_peer(j)) for j in range(1, NN)
    ]
    row_in[n] = row_out[n]

    gat_eh.step3()
    rows_ea.forward()
    rows_dst.forward()

    nodes_down = sublane_iota(N)
    for b in range(blocks):
        piece = slice(b * LANE, (b + 1) * LANE)
        dt[:, piece] = one_hot(nodes_down == jnp.broadcast_to(dstf[:, piece], (N, LANE)))
        slt[:, piece] = one_hot(nodes_down == jnp.broadcast_to(srcf[:, piece], (N, LANE)))

    for copy in halo:
        copy.wait_recv()
    table = jnp.concatenate([lat[...], row_in[...].reshape(NN * PER, LANE)], axis=0)
    rows_src = ToRows(lambda g: ei.at[0, g])
    for j in [*far_first, 0]:
        xx = at_x(j)
        here = pl.ds(xx * RE, RE)
        pick = jnp.concatenate(
            [select_lanes(src_b[here, :], N), select_lanes(q_b[here, :], NN * PER)], axis=1
        )
        srcc[xx] = mm(pick, table).astype(BF)
        rows_src.send(j, srcc.at[xx])
    rows_lat = ToRows(lambda g: ni.at[0, g]).send_all(lambda xx: lat.at[pl.ds(xx * RN, RN), :])
    rows_cot = ToRows(lambda g: cot.at[g]).send_all(lambda xx: nct.at[pl.ds(xx * RN, RN), :])
    for gather in (gat_eo, gat_nh, gat_no):
        gather.step2()

    gat_eh.wait()
    rows_ea.wait()
    rows_dst.wait()
    weh_all = w_eh[...].reshape(3 * L, HC)
    hpre[...] = mm(wide(ei, (1,)), weh_all[L:2 * L]) + mm(wide(ei, (2,)), weh_all[2 * L:])
    gat_eo.step3()
    rows_src.forward()
    rows_src.wait()
    pre = hpre[...] + mm(wide(ei, (0,)), weh_all[:L])
    hpre[...] = pre
    hidden[...] = (pre * jax.nn.sigmoid(pre)).astype(BF)
    gat_eo.wait()
    weo_all = w_eo[...].reshape(L, HC)
    chan_m = ToChan(mm_nt(hidden[...], weo_all), pb_m, rx_m, ch_m)
    gat_nh.step3()
    gat_no.step3()
    chan_m.forward()
    rows_lat.forward()
    rows_cot.forward()
    chan_m.wait()

    fresh = (ea[...].astype(F32) + ch_m[...].reshape(E, LANE).astype(F32)).astype(BF)
    nsum[...] = mm(dt[...], fresh).astype(BF).reshape(NX, RN, LANE)
    rows_sum = ToRows(lambda g: ni.at[1, g]).send_all(lambda xx: nsum.at[xx])

    rows_lat.wait()
    rows_cot.wait()
    gat_nh.wait()
    gat_no.wait()
    wnh_all = w_nh[...].reshape(2 * L, HC)
    cots = wide(cot)
    npre[...] = mm(wide(ni, (0,)), wnh_all[:L])
    pulled = mm(cots, w_no[...].reshape(L, HC))
    rows_sum.forward()
    rows_sum.wait()
    pre = npre[...] + mm(wide(ni, (1,)), wnh_all[L:])
    sig = jax.nn.sigmoid(pre)
    node_hidden = (pre * sig).astype(BF)
    node_back = (pulled * (sig * (1.0 + pre * (1.0 - sig)))).astype(BF)
    chan_n1 = ToChan(mm_nt(node_back, wnh_all[L:]), pb_n.at[1], rx_n.at[1], ch_n.at[1])
    chan_n0 = ToChan(mm_nt(node_back, wnh_all[:L]), pb_n.at[0], rx_n.at[0], ch_n.at[0])
    chan_n1.forward()
    chan_n0.forward()

    def weight_grad(g, values, back):
        per_y = g.shape[1] * g.shape[2]
        for yy in range(NY):
            part = mm_tn(values[:, yy * per_y:(yy + 1) * per_y], back)
            g[yy] = part.astype(BF).reshape(g.shape[1:])

    sc = [Scatter(g, rs_bufs[8 * i:8 * i + 8]) for i, g in enumerate((g_eh, g_nh, g_no, g_eo))]
    sc_eh, sc_nh, sc_no, sc_eo = sc
    weight_grad(g_nh, jnp.concatenate([wide(ni, (0,)), wide(ni, (1,))], axis=1), node_back)
    sc_nh.step1()
    weight_grad(g_no, cots, node_hidden)
    sc_no.step1()

    chan_n1.wait()
    share = ch_n[1].reshape(N, LANE)
    rows_mg = ToRows(lambda g: mg.at[g])
    for j in [*far_first, 0]:
        xx = at_x(j)
        here = pl.ds(xx * RE, RE)
        total = ect[here, :].astype(F32) + mm(select_lanes(dst_b[here, :], N), share)
        ge[here, :] = total
        mgc[xx] = total.astype(BF)
        rows_mg.send(j, mgc.at[xx])
    pre = hpre[...]
    sig = jax.nn.sigmoid(pre)
    hpre[...] = sig * (1.0 + pre * (1.0 - sig))
    rows_mg.forward()
    rows_mg.wait()
    message_grad = wide(mg)
    edge_back = (mm(message_grad, weo_all) * hpre[...]).astype(BF)
    chan_e = [
        ToChan(
            mm_nt(edge_back, weh_all[t * L:(t + 1) * L]), pb_e.at[t], rx_e.at[t], ch_e.at[t]
        )
        for t in range(3)
    ]
    chan_e[0].forward()
    weight_grad(
        g_eh, jnp.concatenate([wide(ei, (t,)) for t in range(3)], axis=1), edge_back
    )
    sc_eh.step1()
    chan_e[1].forward()
    weight_grad(g_eo, message_grad, hidden[...])
    sc_eo.step1()
    chan_e[2].forward()
    sc_nh.step2()
    sc_no.step2()

    chan_e[0].wait()
    from_source = ch_e[0].reshape(E, LANE)
    back = mm(pt[...], from_source).astype(BF)
    for p in range(NN):
        ret_out[p] = back[p * PER:(p + 1) * PER]
    returned = [
        rcopy(ret_out.at[(n + j) % NN], ret_in.at[n], n_peer(j)) for j in range(1, NN)
    ]
    ret_in[n] = ret_out[n]
    sc_nh.step3()
    sc_no.step3()
    chan_n0.wait()
    chan_e[1].wait()
    gl[...] = (
        nct[...].astype(F32)
        + ch_n[0].reshape(N, LANE).astype(F32)
        + mm(slt[...], from_source)
        + mm(dt[...], ch_e[1].reshape(E, LANE))
    )
    sc_eh.step2()
    sc_eo.step2()
    chan_e[2].wait()
    ge[...] = ge[...] + ch_e[2].reshape(E, LANE).astype(F32)
    for copy in returned:
        copy.wait_recv()
    gl[...] = gl[...] + mm_tn(
        rsel[...].reshape(NN * PER, N), ret_in[...].reshape(NN * PER, LANE)
    )
    sc_eh.step3()
    sc_eo.step3()
    out_nh[...] = node_scale * sc_nh.finish()
    out_no[...] = (node_scale * sc_no.finish()).T
    out_eh[...] = edge_scale * sc_eh.finish()
    out_eo[...] = (edge_scale * sc_eo.finish()).T
    flush()


def on_device(
    dims,
    latents, edge_attr, edge_src, edge_dst, send_blocks,
    edge_hidden_w, edge_out_w, node_hidden_w, node_out_w,
    node_cotangent, edge_cotangent,
):
    NX, NY, NZ = dims
    NN = NY * NZ
    E, N = edge_attr.shape[0], latents.shape[0]
    RE, RN = E // NX, N // NX
    G = NX * NC
    L, HC = G * LANE, NX * LANE
    PER = E // 2 // NN

    def v(*shape, dtype=BF):
        return pltpu.VMEM(shape, dtype)

    chunks = [3 * L // NN, 2 * L // NN, L // NN, L // NN]
    rs = []
    for ch in chunks:
        rs += [
            v(NZ - 1, NY, ch, HC // 2), v(NY - 1, NZ, ch, HC // 2),
            v(NY, ch, HC // 2), v(NZ, ch, HC // 2),
            v(NY - 1, ch, HC // 2), v(NZ - 1, ch, HC // 2),
            v(ch, HC), v(NX - 1, ch, LANE),
        ]
    scratch = [
        pltpu.SemaphoreType.DMA((320,)), pltpu.SemaphoreType.DMA((320,)),
        v(3, G, RE, LANE), v(2, G, RN, LANE), v(G, RN, LANE), v(G, RE, LANE),
        v(RE, HC), v(RE, HC, dtype=F32), v(RN, HC, dtype=F32),
        v(E, LANE, dtype=F32), v(E, LANE, dtype=F32), v(E, LANE, dtype=F32),
        v(N, E), v(N, E), v(NN * PER, E), v(NN, PER, N),
        *[v(NN, PER, LANE) for _ in range(6)],
        v(NX, RE, LANE), v(NX, RE, LANE), v(NX, RN, LANE), v(NX, RE, LANE),
        *[v(NY, NZ, ch, HC) for ch in chunks],
        *[v(NY, NZ, ch, HC) for ch in chunks],
        v(NX, NC, RE, LANE), v(NX, RE, LANE), v(NX, RE, LANE),
        v(2, NX, NC, RN, LANE), v(2, NX, RN, LANE), v(2, NX, RN, LANE),
        v(3, NX, NC, RE, LANE), v(3, NX, RE, LANE), v(3, NX, RE, LANE),
        *rs,
    ]
    vmem = pl.BlockSpec(memory_space=pltpu.VMEM)
    smem = pl.BlockSpec(memory_space=pltpu.SMEM)

    def f(*shape):
        return jax.ShapeDtypeStruct(shape, F32)

    return pl.pallas_call(
        functools.partial(kernel, dims),
        out_shape=(
            f(N, LANE), f(E, LANE), f(chunks[0], LANE), f(LANE, chunks[3]),
            f(chunks[1], LANE), f(LANE, chunks[2]),
        ),
        in_specs=[vmem] * 4 + [smem] + [vmem] * 6,
        out_specs=[vmem] * 6,
        scratch_shapes=scratch,
        compiler_params=pltpu.CompilerParams(
            collective_id=0, has_side_effects=True, vmem_limit_bytes=64 * 1024 * 1024 - 65536
        ),
    )(
        latents, edge_attr, edge_src.reshape(1, E), edge_dst.reshape(1, E), send_blocks,
        edge_hidden_w, edge_out_w, node_hidden_w, node_out_w, node_cotangent, edge_cotangent,
    )


def solution(mesh):
    nodes, chans = mesh.shape["node"], mesh.shape["chan"]
    nz = 1
    while nz * nz < nodes:
        nz *= 2
    dims = (chans // NC, nodes // nz, nz)
    return jax.shard_map(
        functools.partial(on_device, dims),
        mesh=mesh,
        in_specs=(
            P("node", "chan"),
            P("node", "chan"),
            P("node"),
            P("node"),
            P("node", None, None),
            P(None, "chan"),
            P("chan", None),
            P(None, "chan"),
            P("chan", None),
            P("node", "chan"),
            P("node", "chan"),
        ),
        out_specs=(
            P("node", "chan"),
            P("node", "chan"),
            P("node", "chan"),
            P("chan", "node"),
            P("node", "chan"),
            P("chan", "node"),
        ),
        check_vma=False,
    )
```

```python
import functools

import jax
import jax.numpy as jnp
from jax import lax
from jax.experimental import pallas as pl
from jax.experimental.pallas import tpu as pltpu
from jax.sharding import PartitionSpec as P

BF = jnp.bfloat16
F32 = jnp.float32
LANE = 128
NC = 2


def mm(a, b):
    return jnp.dot(a, b, preferred_element_type=F32)


def mm_nt(a, b):
    return lax.dot_general(a, b, (((1,), (1,)), ((), ())), preferred_element_type=F32)


def mm_tn(a, b):
    return lax.dot_general(a, b, (((0,), (0,)), ((), ())), preferred_element_type=F32)


def one_hot(mask):
    return jnp.where(mask, 1.0, 0.0).astype(BF)


def lane_iota(rows):
    return lax.broadcasted_iota(jnp.int32, (rows, LANE), 1).astype(F32)


def sublane_iota(rows):
    return lax.broadcasted_iota(jnp.int32, (rows, LANE), 0).astype(F32)


def select_lanes(index, width):
    lanes = lane_iota(index.shape[0])
    return jnp.concatenate(
        [one_hot(index == lanes + float(b * LANE)) for b in range(width // LANE)], axis=1
    )


def wide(ref, lead=()):
    groups = ref.shape[len(lead)]
    return jnp.concatenate([ref[(*lead, g)] for g in range(groups)], axis=1)


def kernel(
    dims,
    lat_hbm, ea_hbm, src, dst, sb, weh, weo_hbm, wnh, wno_hbm, nct_hbm, ect_hbm,
    gl_hbm, ge_hbm, out_eh, out_eo, out_nh, out_no,
    ssem, rsem, lsem,
    lat, ea, weo, wno, nct, ect, gl, ge,
    ei, ni, cot, mg, hidden, hpre, npre,
    src_b, dst_b, q_b, dt, slt, pt, rsel,
    rq_out, rq_in, row_out, row_in, ret_out, ret_in,
    srcc, dstc, nsum, mgc,
    w_eh, w_nh, w_no, w_eo,
    g_eh, g_nh, g_no, g_eo,
    pb_m, rx_m, ch_m, pb_n, rx_n, ch_n, pb_e, rx_e, ch_e,
    *rs_bufs,
):
    NX, NY, NZ = dims
    NN = NY * NZ
    E, N = ea.shape[0], lat.shape[0]
    RE, RN = E // NX, N // NX
    L = NX * NC * LANE
    HC = NX * LANE
    PER = E // 2 // NN
    SLOT = PER // 2
    edge_scale = float(E * NN) ** (-0.5)
    node_scale = float(N * NN) ** (-0.5)

    n, k = lax.axis_index("node"), lax.axis_index("chan")
    x, c = k // NC, k % NC
    y, z = n // NZ, n % NZ

    def at_x(j):
        return (x + j) % NX

    def x_peer(j):
        return (n, at_x(j) * NC + c)

    def y_peer(j):
        return (((y + j) % NY) * NZ + z, k)

    def z_peer(j):
        return (y * NZ + (z + j) % NZ, k)

    def n_peer(j):
        return ((n + j) % NN, k)

    sib = (n, x * NC + 1 - c)

    pending = []
    used = [0]

    def rcopy(a, b, device):
        i = used[0]
        used[0] += 1
        copy = pltpu.make_async_remote_copy(
            src_ref=a, dst_ref=b, send_sem=ssem.at[i], recv_sem=rsem.at[i],
            device_id=device, device_id_type=pl.DeviceIdType.MESH,
        )
        copy.start()
        pending.append(copy)
        return copy

    def flush():
        while pending:
            pending.pop(0).wait_send()

    far_first = sorted(range(1, NX), key=lambda j: -min(j, NX - j))

    class ToRows:
        def __init__(self, put):
            self.put, self.near, self.far = put, [], []

        def send(self, j, chunk):
            if j:
                self.far.append((j, rcopy(chunk, self.put(x * NC + c), x_peer(j))))
            else:
                self.put(x * NC + c)[...] = chunk[...]
                self.near.append(rcopy(chunk, self.put(x * NC + c), sib))
            return self

        def send_all(self, chunk):
            for j in [*far_first, 0]:
                self.send(j, chunk(at_x(j)))
            return self

        def forward(self):
            for j, copy in self.far:
                copy.wait_recv()
                slot = self.put(at_x(NX - j) * NC + c)
                self.near.append(rcopy(slot, slot, sib))

        def wait(self):
            for copy in self.near:
                copy.wait_recv()

    class ToChan:
        def __init__(self, value, pb, rx, ch):
            self.pb, self.rx, self.ch, self.far = pb, rx, ch, []
            for g in range(NX * NC):
                pb[g // NC, g % NC] = value[:, g * LANE:(g + 1) * LANE].astype(BF)
            self.near = [
                (j, rcopy(pb.at[at_x(j), 1 - c], rx.at[at_x(j)], sib)) for j in [*far_first, 0]
            ]

        def forward(self):
            for j, copy in self.near:
                copy.wait_recv()
                xx = at_x(j)
                total = (self.rx[xx].astype(F32) + self.pb[xx, c].astype(F32)).astype(BF)
                if j:
                    self.rx[xx] = total
                    self.far.append(rcopy(self.rx.at[xx], self.ch.at[x], x_peer(j)))
                else:
                    self.ch[x] = total

        def wait(self):
            for copy in self.far:
                copy.wait_recv()

    class Gather:
        def __init__(self, w):
            self.w, self.half = w, w.shape[2] // 2

        def step1(self, own):
            w = self.w
            self.copies = [
                rcopy(own, w.at[y, z, :, pl.ds((NX - j) * LANE, LANE)], x_peer(j))
                for j in range(1, NX)
            ]

        def _recv(self):
            for copy in self.copies:
                copy.wait_recv()

        def step2(self):
            self._recv()
            w, h = self.w, self.half
            a = w.at[y, z, pl.ds(0, h), pl.ds(LANE, HC - LANE)]
            b = w.at[y, z, pl.ds(h, h), pl.ds(LANE, HC - LANE)]
            self.copies = [rcopy(a, a, z_peer(j)) for j in range(1, NZ)]
            self.copies += [rcopy(b, b, y_peer(j)) for j in range(1, NY)]

        def step3(self):
            self._recv()
            w, h = self.w, self.half
            rest = pl.ds(LANE, HC - LANE)
            self.rings = [
                (lambda yy, part: w.at[yy, part, pl.ds(0, h), rest], y, NY, y_peer, NZ),
                (lambda zz, part: w.at[part, zz, pl.ds(h, h), rest], z, NZ, z_peer, NY),
            ]
            self.copies = []
            for place, me, size, peer, across in self.rings:
                mine = place(me, pl.ds(0, across))
                self.copies.append([
                    rcopy(mine, mine, peer(j)) for j in sorted({1, size - 1})
                ])

        def step4(self):
            sent, self.copies = self.copies, []
            for (place, me, size, peer, across), ring in zip(self.rings, sent):
                if size == 2:
                    self.copies += ring
                    continue
                part = across // 2
                for copy, j, first in ((ring[0], 1, 0), (ring[1], size - 1, part)):
                    copy.wait_recv()
                    passed = place((me + size - j) % size, pl.ds(first, part))
                    self.copies.append(rcopy(passed, passed, peer(j)))

        def wait(self):
            self._recv()

    class Scatter:
        def __init__(self, g, bufs, over_x=False):
            self.g = g
            self.ra, self.rb, self.sa, self.sbb, self.ra2, self.rb2, self.s2, self.r3 = bufs[:8]
            self.main = self.s2.shape[0]
            self.over_x = over_x
            if over_x:
                self.rx1, self.sx, self.rx2, self.sx2, self.rx3 = bufs[8:]
            half, rows = HC // 2, pl.ds(0, self.main)
            self.rings = (
                (lambda d, part: (part, (z + d) % NZ, rows, pl.ds(0, half)),
                 self.ra, NZ, z_peer, NY),
                (lambda d, part: ((y + d) % NY, part, rows, pl.ds(half, half)),
                 self.rb, NY, y_peer, NZ),
            )

        def step1(self):
            self.relay, self.full = [], []
            for index, land, size, peer, across in self.rings:
                part = across // 2
                lo, hi = pl.ds(0, part), pl.ds(part, part)
                if size == 2:
                    continue
                self.relay.append([
                    rcopy(self.g.at[index(2, lo)], land.at[1, lo], peer(1)),
                    rcopy(self.g.at[index(2, hi)], land.at[1, hi], peer(3)),
                ])

        def step1b(self):
            for index, land, size, peer, across in self.rings:
                part = across // 2
                lo, hi = pl.ds(0, part), pl.ds(part, part)
                if size == 2:
                    every = pl.ds(0, across)
                    self.full.append([rcopy(self.g.at[index(1, every)], land.at[0], peer(1))])
                else:
                    self.full.append([
                        rcopy(self.g.at[index(1, hi)], land.at[0, hi], peer(1)),
                        rcopy(self.g.at[index(3, lo)], land.at[2, lo], peer(3)),
                    ])
            if self.over_x:
                part = pl.ds(self.main, self.g.shape[2] - self.main)
                self.xs = [
                    rcopy(
                        self.g.at[:, :, part, pl.ds(j * LANE, LANE)], self.rx1.at[j - 1], x_peer(j)
                    )
                    for j in range(1, NX)
                ]

        def step1c(self):
            for (index, land, size, peer, across), relay, full in zip(
                self.rings, self.relay, self.full
            ):
                part = across // 2
                for copy, j, here in (
                    (relay[0], 1, pl.ds(0, part)), (relay[1], 3, pl.ds(part, part))
                ):
                    copy.wait_recv()
                    at = index(j, here)
                    self.g[at] = (
                        self.g[at].astype(F32) + land[1, here].astype(F32)
                    ).astype(BF)
                    full.append(rcopy(self.g.at[at], land.at[j - 1, here], peer(j)))

        def step2(self):
            g, half, m = self.g, HC // 2, self.main
            for copy in self.full[0]:
                copy.wait_recv()
            for yy in range(NY):
                total = g[yy, z, 0:m, 0:half].astype(F32)
                for j in sorted({1, NZ - 1}):
                    total = total + self.ra[j - 1, yy].astype(F32)
                self.sa[yy] = total.astype(BF)
            self.a = [
                rcopy(self.sa.at[(y + j) % NY], self.ra2.at[j - 1], y_peer(j))
                for j in range(1, NY)
            ]
            for copy in self.full[1]:
                copy.wait_recv()
            for zz in range(NZ):
                total = g[y, zz, 0:m, half:HC].astype(F32)
                for j in sorted({1, NY - 1}):
                    total = total + self.rb[j - 1, zz].astype(F32)
                self.sbb[zz] = total.astype(BF)
            self.b = [
                rcopy(self.sbb.at[(z + j) % NZ], self.rb2.at[j - 1], z_peer(j))
                for j in range(1, NZ)
            ]

        def x_step2(self):
            for copy in self.xs:
                copy.wait_recv()
            for yy in range(NY):
                total = self.g[yy, :, self.main:, 0:LANE].astype(F32)
                for j in range(1, NX):
                    total = total + self.rx1[j - 1, yy].astype(F32)
                self.sx[yy] = total.astype(BF)
            self.xs = [
                rcopy(self.sx.at[:, (z + j) % NZ], self.rx2.at[j - 1], z_peer(j))
                for j in range(1, NZ)
            ]

        def x_step3(self):
            for copy in self.xs:
                copy.wait_recv()
            total = self.sx[:, z].astype(F32)
            for j in range(1, NZ):
                total = total + self.rx2[j - 1].astype(F32)
            self.sx2[...] = total.astype(BF)
            self.xs = [
                rcopy(self.sx2.at[(y + j) % NY], self.rx3.at[j - 1], y_peer(j))
                for j in range(1, NY)
            ]

        def x_finish(self):
            for copy in self.xs:
                copy.wait_recv()
            total = self.sx2[y].astype(F32)
            for j in range(1, NY):
                total = total + self.rx3[j - 1].astype(F32)
            return total

        def step3(self):
            half = HC // 2
            for copy in self.a:
                copy.wait_recv()
            total = self.sa[y].astype(F32)
            for j in range(1, NY):
                total = total + self.ra2[j - 1].astype(F32)
            self.s2[:, 0:half] = total.astype(BF)
            for copy in self.b:
                copy.wait_recv()
            total = self.sbb[z].astype(F32)
            for j in range(1, NZ):
                total = total + self.rb2[j - 1].astype(F32)
            self.s2[:, half:HC] = total.astype(BF)
            self.x = [
                rcopy(self.s2.at[:, pl.ds(j * LANE, LANE)], self.r3.at[j - 1], x_peer(j))
                for j in range(1, NX)
            ]

        def finish(self):
            for copy in self.x:
                copy.wait_recv()
            total = self.s2[:, 0:LANE].astype(F32)
            for j in range(1, NX):
                total = total + self.r3[j - 1].astype(F32)
            return total

    def local(a, b, i):
        copy = pltpu.make_async_copy(a, b, lsem.at[i])
        copy.start()
        return copy

    barrier = pltpu.get_barrier_semaphore()
    partners = [x_peer(j) for j in range(1, NX)] + [sib] + [n_peer(j) for j in range(1, NN)]
    for device in partners:
        pl.semaphore_signal(barrier, inc=1, device_id=device, device_id_type=pl.DeviceIdType.MESH)
    get_lat, get_weo, get_wno, get_weh, get_wnh, get_ea, get_nct, get_ect = [
        local(a, b, i)
        for i, (a, b) in enumerate((
            (lat_hbm, lat), (weo_hbm, weo), (wno_hbm, wno),
            (weh, w_eh.at[:, :, :, pl.ds(0, LANE)]), (wnh, w_nh.at[:, :, :, pl.ds(0, LANE)]),
            (ea_hbm, ea), (nct_hbm, nct), (ect_hbm, ect),
        ))
    ]

    srcf = src[...].reshape(1, E).astype(F32)
    dstf = dst[...].reshape(1, E).astype(F32)
    is_far = srcf >= float(N)
    slotf = jnp.where(is_far, jnp.floor((srcf - float(N)) * (1.0 / LANE)), -1.0)
    blocks = E // LANE
    for b in range(blocks):
        piece = slice(b * LANE, (b + 1) * LANE)
        src_b[piece, :] = jnp.broadcast_to(srcf[:, piece], (LANE, LANE)).T
        dst_b[piece, :] = jnp.broadcast_to(dstf[:, piece], (LANE, LANE)).T
    src_col = src_b[...]
    slot_col = jnp.where(
        src_col >= float(N), jnp.floor((src_col - float(N)) * (1.0 / LANE)), -1.0
    )
    order = sublane_iota(E)
    place = sublane_iota(NN * PER)
    for b in range(blocks):
        piece = slice(b * LANE, (b + 1) * LANE)
        mine = jnp.broadcast_to(slotf[:, piece], (E, LANE))
        before = (slot_col == mine) & (order < lane_iota(E) + float(b * LANE))
        rank = jnp.sum(jnp.where(before, 1.0, 0.0), axis=0, keepdims=True)
        q = jnp.where(is_far[:, piece], slotf[:, piece] * float(SLOT) + rank, -1.0)
        pt[:, piece] = one_hot(place == jnp.broadcast_to(q, (NN * PER, LANE)))
        q_b[piece, :] = jnp.broadcast_to(q, (LANE, LANE)).T
    row_in_block = (src_col - LANE * jnp.floor(src_col * (1.0 / LANE))).astype(BF)
    wanted = mm(pt[...], row_in_block).astype(BF)
    for p in range(NN):
        rq_out[p] = wanted[p * PER:(p + 1) * PER]
    get_weo.wait()
    get_wno.wait()
    w_eo[:, :, :, 0:LANE] = weo[...].T.reshape(NY, NZ, L // NN, LANE)
    w_no[:, :, :, 0:LANE] = wno[...].T.reshape(NY, NZ, L // NN, LANE)
    pl.semaphore_wait(barrier, len(partners))

    gat_eh, gat_nh, gat_no, gat_eo = Gather(w_eh), Gather(w_nh), Gather(w_no), Gather(w_eo)
    gat_eh.step1(weh.at[y, z])
    ask = [
        rcopy(rq_out.at[(n + j) % NN], rq_in.at[n], n_peer(j)) for j in range(1, NN)
    ]
    rq_in[n] = rq_out[n]
    get_lat.wait()
    get_ea.wait()
    rows_ea = ToRows(lambda g: ei.at[2, g]).send_all(lambda xx: ea.at[pl.ds(xx * RE, RE), :])
    gat_eo.step1(w_eo.at[y, z, :, pl.ds(0, LANE)])
    gat_nh.step1(wnh.at[y, z])
    gat_no.step1(w_no.at[y, z, :, pl.ds(0, LANE)])

    rows_dst = ToRows(lambda g: ei.at[1, g])
    for j in [*far_first, 0]:
        xx = at_x(j)
        pick = select_lanes(dst_b[pl.ds(xx * RE, RE), :], N)
        dstc[xx] = mm(pick, lat[...]).astype(BF)
        rows_dst.send(j, dstc.at[xx])

    gat_eh.step2()

    for copy in ask:
        copy.wait_recv()
    half_rows = sublane_iota(PER) < float(SLOT)
    for d in range(NN):
        base = jnp.where(
            half_rows,
            (sb[0, d] * LANE).astype(F32),
            (sb[1, d] * LANE).astype(F32),
        )
        rsel[d] = select_lanes(rq_in[d].astype(F32) + base, N)
    given = mm(rsel[...].reshape(NN * PER, N), lat[...]).astype(BF)
    for d in range(NN):
        row_out[d] = given[d * PER:(d + 1) * PER]
    halo = [
        rcopy(row_out.at[(n + j) % NN], row_in.at[n], n_peer(j)) for j in range(1, NN)
    ]
    row_in[n] = row_out[n]

    gat_eo.step2()
    gat_eh.step3()
    rows_ea.forward()
    rows_dst.forward()
    gat_nh.step2()
    gat_no.step2()

    nodes_down = sublane_iota(N)
    for b in range(blocks):
        piece = slice(b * LANE, (b + 1) * LANE)
        dt[:, piece] = one_hot(nodes_down == jnp.broadcast_to(dstf[:, piece], (N, LANE)))
        slt[:, piece] = one_hot(nodes_down == jnp.broadcast_to(srcf[:, piece], (N, LANE)))

    gat_eo.step3()
    gat_eh.step4()

    for copy in halo:
        copy.wait_recv()
    table = jnp.concatenate([lat[...], row_in[...].reshape(NN * PER, LANE)], axis=0)
    rows_src = ToRows(lambda g: ei.at[0, g])
    for j in [*far_first, 0]:
        xx = at_x(j)
        here = pl.ds(xx * RE, RE)
        pick = jnp.concatenate(
            [select_lanes(src_b[here, :], N), select_lanes(q_b[here, :], NN * PER)], axis=1
        )
        srcc[xx] = mm(pick, table).astype(BF)
        rows_src.send(j, srcc.at[xx])
    gat_nh.step3()
    gat_no.step3()
    gat_eo.step4()

    get_weh.wait()
    gat_eh.wait()
    rows_ea.wait()
    rows_dst.wait()
    weh_all = w_eh[...].reshape(3 * L, HC)
    hpre[...] = mm(wide(ei, (1,)), weh_all[L:2 * L]) + mm(wide(ei, (2,)), weh_all[2 * L:])
    rows_src.forward()
    get_nct.wait()
    rows_lat = ToRows(lambda g: ni.at[0, g]).send_all(lambda xx: lat.at[pl.ds(xx * RN, RN), :])
    rows_cot = ToRows(lambda g: cot.at[g]).send_all(lambda xx: nct.at[pl.ds(xx * RN, RN), :])
    gat_nh.step4()
    gat_no.step4()
    rows_src.wait()
    pre = hpre[...] + mm(wide(ei, (0,)), weh_all[:L])
    hpre[...] = pre
    hidden[...] = (pre * jax.nn.sigmoid(pre)).astype(BF)
    gat_eo.wait()
    weo_all = w_eo[...].reshape(L, HC)
    chan_m = ToChan(mm_nt(hidden[...], weo_all), pb_m, rx_m, ch_m)
    chan_m.forward()
    rows_lat.forward()
    rows_cot.forward()
    chan_m.wait()

    fresh = (ea[...].astype(F32) + ch_m[...].reshape(E, LANE).astype(F32)).astype(BF)
    nsum[...] = mm(dt[...], fresh).astype(BF).reshape(NX, RN, LANE)
    rows_sum = ToRows(lambda g: ni.at[1, g]).send_all(lambda xx: nsum.at[xx])

    rows_lat.wait()
    rows_cot.wait()
    get_wnh.wait()
    gat_nh.wait()
    gat_no.wait()
    wnh_all = w_nh[...].reshape(2 * L, HC)
    cots = wide(cot)
    npre[...] = mm(wide(ni, (0,)), wnh_all[:L])
    pulled = mm(cots, w_no[...].reshape(L, HC))
    rows_sum.forward()
    rows_sum.wait()
    pre = npre[...] + mm(wide(ni, (1,)), wnh_all[L:])
    sig = jax.nn.sigmoid(pre)
    node_hidden = (pre * sig).astype(BF)
    node_back = (pulled * (sig * (1.0 + pre * (1.0 - sig)))).astype(BF)
    chan_n1 = ToChan(mm_nt(node_back, wnh_all[L:]), pb_n.at[1], rx_n.at[1], ch_n.at[1])
    chan_n0 = ToChan(mm_nt(node_back, wnh_all[:L]), pb_n.at[0], rx_n.at[0], ch_n.at[0])
    chan_n1.forward()
    chan_n0.forward()

    def weight_grad(g, values, back):
        per_y = g.shape[1] * g.shape[2]
        for yy in range(NY):
            part = mm_tn(values[:, yy * per_y:(yy + 1) * per_y], back)
            g[yy] = part.astype(BF).reshape(g.shape[1:])

    sc_eh, sc_eo = Scatter(g_eh, rs_bufs[0:13], True), Scatter(g_eo, rs_bufs[13:26], True)
    sc_nh, sc_no = Scatter(g_nh, rs_bufs[26:34]), Scatter(g_no, rs_bufs[34:42])
    weight_grad(g_nh, jnp.concatenate([wide(ni, (0,)), wide(ni, (1,))], axis=1), node_back)
    sc_nh.step1()
    weight_grad(g_no, cots, node_hidden)
    sc_no.step1()
    sc_nh.step1b()
    sc_no.step1b()

    chan_n1.wait()
    share = ch_n[1].reshape(N, LANE)
    get_ect.wait()
    rows_mg = ToRows(lambda g: mg.at[g])
    for j in [*far_first, 0]:
        xx = at_x(j)
        here = pl.ds(xx * RE, RE)
        total = ect[here, :].astype(F32) + mm(select_lanes(dst_b[here, :], N), share)
        ge[here, :] = total
        mgc[xx] = total.astype(BF)
        rows_mg.send(j, mgc.at[xx])
    pre = hpre[...]
    sig = jax.nn.sigmoid(pre)
    hpre[...] = sig * (1.0 + pre * (1.0 - sig))
    rows_mg.forward()
    sc_nh.step1c()
    sc_no.step1c()
    rows_mg.wait()
    message_grad = wide(mg)
    edge_back = (mm(message_grad, weo_all) * hpre[...]).astype(BF)
    chan_e = [
        ToChan(
            mm_nt(edge_back, weh_all[t * L:(t + 1) * L]), pb_e.at[t], rx_e.at[t], ch_e.at[t]
        )
        for t in range(3)
    ]
    chan_e[0].forward()
    weight_grad(
        g_eh, jnp.concatenate([wide(ei, (t,)) for t in range(3)], axis=1), edge_back
    )
    sc_eh.step1()
    chan_e[1].forward()
    weight_grad(g_eo, message_grad, hidden[...])
    sc_eo.step1()
    sc_nh.step2()
    sc_no.step2()
    chan_e[2].forward()
    sc_eh.step1b()
    sc_eo.step1b()

    chan_e[0].wait()
    from_source = ch_e[0].reshape(E, LANE)
    back = mm(pt[...], from_source).astype(BF)
    for p in range(NN):
        ret_out[p] = back[p * PER:(p + 1) * PER]
    returned = [
        rcopy(ret_out.at[(n + j) % NN], ret_in.at[n], n_peer(j)) for j in range(1, NN)
    ]
    ret_in[n] = ret_out[n]
    sc_eh.step1c()
    sc_eo.step1c()
    sc_nh.step3()
    sc_no.step3()
    chan_n0.wait()
    chan_e[1].wait()
    gl[...] = (
        nct[...].astype(F32)
        + ch_n[0].reshape(N, LANE).astype(F32)
        + mm(slt[...], from_source)
        + mm(dt[...], ch_e[1].reshape(E, LANE))
    )
    chan_e[2].wait()
    ge[...] = ge[...] + ch_e[2].reshape(E, LANE).astype(F32)
    put_ge = local(ge, ge_hbm, 8)
    for copy in returned:
        copy.wait_recv()
    gl[...] = gl[...] + mm_tn(
        rsel[...].reshape(NN * PER, N), ret_in[...].reshape(NN * PER, LANE)
    )
    put_gl = local(gl, gl_hbm, 9)
    out_nh[...] = node_scale * sc_nh.finish()
    out_no[...] = node_scale * sc_no.finish()
    for step in ("x_step2", "step2", "x_step3", "step3"):
        for scatter in (sc_eh, sc_eo):
            getattr(scatter, step)()
    for scatter, out in ((sc_eh, out_eh), (sc_eo, out_eo)):
        out[scatter.main:, :] = edge_scale * scatter.x_finish()
        out[:scatter.main, :] = edge_scale * scatter.finish()
    put_ge.wait()
    put_gl.wait()
    flush()


def hand_over(*refs):
    count = (len(refs) - 2) // 3
    given, taken, held = refs[:count], refs[count:2 * count], refs[2 * count:3 * count]
    in_sem, out_sem = refs[3 * count:]
    loads = [
        pltpu.make_async_copy(a, b, in_sem.at[i]) for i, (a, b) in enumerate(zip(given, held))
    ]
    stores = [
        pltpu.make_async_copy(a, b, out_sem.at[i]) for i, (a, b) in enumerate(zip(held, taken))
    ]
    for load in loads:
        load.start()
    for load, store in zip(loads, stores):
        load.wait()
        store.start()
    for store in stores:
        store.wait()


def on_device(
    dims,
    latents, edge_attr, edge_src, edge_dst, send_blocks,
    edge_hidden_w, edge_out_w, node_hidden_w, node_out_w,
    node_cotangent, edge_cotangent,
):
    NX, NY, NZ = dims
    NN = NY * NZ
    E, N = edge_attr.shape[0], latents.shape[0]
    RE, RN = E // NX, N // NX
    G = NX * NC
    L, HC = G * LANE, NX * LANE
    PER = E // 2 // NN

    def v(*shape, dtype=BF):
        return pltpu.VMEM(shape, dtype)

    chunks = [3 * L // NN, 2 * L // NN, L // NN, L // NN]
    rs = []
    for i in (0, 3, 1, 2):
        part = max(16, chunks[i] // 4 // 16 * 16) if i in (0, 3) else 0
        ch = chunks[i] - part
        rs += [
            v(NZ - 1, NY, ch, HC // 2), v(NY - 1, NZ, ch, HC // 2),
            v(NY, ch, HC // 2), v(NZ, ch, HC // 2),
            v(NY - 1, ch, HC // 2), v(NZ - 1, ch, HC // 2),
            v(ch, HC), v(NX - 1, ch, LANE),
        ]
        if part:
            rs += [
                v(NX - 1, NY, NZ, part, LANE), v(NY, NZ, part, LANE),
                v(NZ - 1, NY, part, LANE), v(NY, part, LANE), v(NY - 1, part, LANE),
            ]
    scratch = [
        pltpu.SemaphoreType.DMA((320,)), pltpu.SemaphoreType.DMA((320,)),
        pltpu.SemaphoreType.DMA((10,)),
        v(N, LANE), v(E, LANE), v(LANE, L), v(LANE, L), v(N, LANE), v(E, LANE),
        v(N, LANE, dtype=F32), v(E, LANE, dtype=F32),
        v(3, G, RE, LANE), v(2, G, RN, LANE), v(G, RN, LANE), v(G, RE, LANE),
        v(RE, HC), v(RE, HC, dtype=F32), v(RN, HC, dtype=F32),
        v(E, LANE, dtype=F32), v(E, LANE, dtype=F32), v(E, LANE, dtype=F32),
        v(N, E), v(N, E), v(NN * PER, E), v(NN, PER, N),
        *[v(NN, PER, LANE) for _ in range(6)],
        v(NX, RE, LANE), v(NX, RE, LANE), v(NX, RN, LANE), v(NX, RE, LANE),
        *[v(NY, NZ, ch, HC) for ch in chunks],
        *[v(NY, NZ, ch, HC) for ch in chunks],
        v(NX, NC, RE, LANE), v(NX, RE, LANE), v(NX, RE, LANE),
        v(2, NX, NC, RN, LANE), v(2, NX, RN, LANE), v(2, NX, RN, LANE),
        v(3, NX, NC, RE, LANE), v(3, NX, RE, LANE), v(3, NX, RE, LANE),
        *rs,
    ]
    vmem = pl.BlockSpec(memory_space=pltpu.VMEM)
    smem = pl.BlockSpec(memory_space=pltpu.SMEM)
    hbm = pl.BlockSpec(memory_space=pl.ANY)

    def f(*shape):
        return jax.ShapeDtypeStruct(shape, F32)

    results = pl.pallas_call(
        functools.partial(kernel, dims),
        out_shape=(
            f(N, LANE), f(E, LANE), f(chunks[0], LANE), f(chunks[3], LANE),
            f(chunks[1], LANE), f(chunks[2], LANE),
        ),
        in_specs=[hbm, hbm, vmem, vmem, smem] + [hbm] * 6,
        out_specs=[hbm, hbm] + [vmem] * 4,
        scratch_shapes=scratch,
        compiler_params=pltpu.CompilerParams(
            collective_id=0, has_side_effects=True, vmem_limit_bytes=64 * 1024 * 1024 - 65536
        ),
    )(
        latents, edge_attr, edge_src, edge_dst, send_blocks[0].T,
        edge_hidden_w.reshape(NY, NZ, chunks[0], LANE), edge_out_w,
        node_hidden_w.reshape(NY, NZ, chunks[1], LANE), node_out_w,
        node_cotangent, edge_cotangent,
    )
    gl, ge, g_eh, g_eo, g_nh, g_no = pl.pallas_call(
        hand_over,
        out_shape=tuple(jax.ShapeDtypeStruct(r.shape, r.dtype) for r in results),
        in_specs=[hbm] * 6,
        out_specs=[hbm] * 6,
        scratch_shapes=[
            *[pltpu.VMEM(r.shape, r.dtype) for r in results],
            pltpu.SemaphoreType.DMA((6,)), pltpu.SemaphoreType.DMA((6,)),
        ],
        compiler_params=pltpu.CompilerParams(vmem_limit_bytes=60 * 1024 * 1024),
    )(*results)
    return gl, ge, g_eh, g_eo.T, g_nh, g_no.T


def solution(mesh):
    nodes, chans = mesh.shape["node"], mesh.shape["chan"]
    nz = 1
    while nz * nz < nodes:
        nz *= 2
    dims = (chans // NC, nodes // nz, nz)
    return jax.shard_map(
        functools.partial(on_device, dims),
        mesh=mesh,
        in_specs=(
            P("node", "chan"),
            P("node", "chan"),
            P("node"),
            P("node"),
            P("node", None, None),
            P(None, "chan"),
            P("chan", None),
            P(None, "chan"),
            P("chan", None),
            P("node", "chan"),
            P("node", "chan"),
        ),
        out_specs=(
            P("node", "chan"),
            P("node", "chan"),
            P("node", "chan"),
            P("chan", "node"),
            P("node", "chan"),
            P("chan", "node"),
        ),
        check_vma=False,
    )
```

```python
import functools

import jax
import jax.numpy as jnp
from jax import lax
from jax.experimental import pallas as pl
from jax.experimental.pallas import tpu as pltpu
from jax.sharding import PartitionSpec as P

BF = jnp.bfloat16
F32 = jnp.float32
LANE = 128
NC = 2


def mm(a, b):
    return jnp.dot(a, b, preferred_element_type=F32)


def mm_nt(a, b):
    return lax.dot_general(a, b, (((1,), (1,)), ((), ())), preferred_element_type=F32)


def mm_tn(a, b):
    return lax.dot_general(a, b, (((0,), (0,)), ((), ())), preferred_element_type=F32)


def one_hot(mask):
    return jnp.where(mask, 1.0, 0.0).astype(BF)


def lane_iota(rows):
    return lax.broadcasted_iota(jnp.int32, (rows, LANE), 1).astype(F32)


def sublane_iota(rows):
    return lax.broadcasted_iota(jnp.int32, (rows, LANE), 0).astype(F32)


def select_lanes(index, width):
    lanes = lane_iota(index.shape[0])
    return jnp.concatenate(
        [one_hot(index == lanes + float(b * LANE)) for b in range(width // LANE)], axis=1
    )


def wide(ref, lead=()):
    groups = ref.shape[len(lead)]
    return jnp.concatenate([ref[(*lead, g)] for g in range(groups)], axis=1)


def kernel(
    dims,
    lat_hbm, ea_hbm, src, dst, sb, weh, weo_hbm, wnh, wno_hbm, nct_hbm, ect_hbm,
    gl_hbm, ge_hbm, out_eh, out_eo, out_nh, out_no,
    ssem, rsem, lsem,
    lat, ea, weo, wno, nct, ect, gl, ge,
    ei, ni, cot, mg, hidden, hpre, npre,
    src_b, dst_b, q_b, dt, slt, pt, rsel,
    rq_out, rq_in, row_out, row_in, ret_out, ret_in,
    srcc, dstc, nsum, mgc,
    w_eh, w_nh, w_no, w_eo,
    g_eh, g_nh, g_no, g_eo,
    pb_m, rx_m, ch_m, pb_n, rx_n, ch_n, pb_e, rx_e, ch_e,
    *rs_bufs,
):
    NX, NY, NZ = dims
    NN = NY * NZ
    E, N = ea.shape[0], lat.shape[0]
    RE, RN = E // NX, N // NX
    L = NX * NC * LANE
    HC = NX * LANE
    PER = E // 2 // NN
    SLOT = PER // 2
    edge_scale = float(E * NN) ** (-0.5)
    node_scale = float(N * NN) ** (-0.5)

    n, k = lax.axis_index("node"), lax.axis_index("chan")
    x, c = k // NC, k % NC
    y, z = n // NZ, n % NZ

    def at_x(j):
        return (x + j) % NX

    def x_peer(j):
        return (n, at_x(j) * NC + c)

    def y_peer(j):
        return (((y + j) % NY) * NZ + z, k)

    def z_peer(j):
        return (y * NZ + (z + j) % NZ, k)

    def n_peer(j):
        return ((n + j) % NN, k)

    sib = (n, x * NC + 1 - c)

    pending = []
    used = [0]

    def rcopy(a, b, device):
        i = used[0]
        used[0] += 1
        copy = pltpu.make_async_remote_copy(
            src_ref=a, dst_ref=b, send_sem=ssem.at[i], recv_sem=rsem.at[i],
            device_id=device, device_id_type=pl.DeviceIdType.MESH,
        )
        copy.start()
        pending.append(copy)
        return copy

    def flush():
        while pending:
            pending.pop(0).wait_send()

    far_first = sorted(range(1, NX), key=lambda j: -min(j, NX - j))

    class ToRows:
        def __init__(self, put):
            self.put, self.near, self.far = put, [], []

        def send(self, j, chunk):
            if j:
                self.far.append((j, rcopy(chunk, self.put(x * NC + c), x_peer(j))))
            else:
                self.put(x * NC + c)[...] = chunk[...]
                self.near.append(rcopy(chunk, self.put(x * NC + c), sib))
            return self

        def send_all(self, chunk):
            for j in [*far_first, 0]:
                self.send(j, chunk(at_x(j)))
            return self

        def forward(self):
            for j, copy in self.far:
                copy.wait_recv()
                slot = self.put(at_x(NX - j) * NC + c)
                self.near.append(rcopy(slot, slot, sib))

        def wait(self):
            for copy in self.near:
                copy.wait_recv()

    class ToChan:
        def __init__(self, value, pb, rx, ch):
            self.pb, self.rx, self.ch, self.far = pb, rx, ch, []
            for g in range(NX * NC):
                pb[g // NC, g % NC] = value[:, g * LANE:(g + 1) * LANE].astype(BF)
            self.near = [
                (j, rcopy(pb.at[at_x(j), 1 - c], rx.at[at_x(j)], sib)) for j in [*far_first, 0]
            ]

        def forward(self):
            for j, copy in self.near:
                copy.wait_recv()
                xx = at_x(j)
                total = (self.rx[xx].astype(F32) + self.pb[xx, c].astype(F32)).astype(BF)
                if j:
                    self.rx[xx] = total
                    self.far.append(rcopy(self.rx.at[xx], self.ch.at[x], x_peer(j)))
                else:
                    self.ch[x] = total

        def wait(self):
            for copy in self.far:
                copy.wait_recv()

    class Gather:
        def __init__(self, w):
            self.w, self.half = w, w.shape[2] // 2

        def step1(self, own):
            w = self.w
            self.copies = [
                rcopy(own, w.at[y, z, :, pl.ds((NX - j) * LANE, LANE)], x_peer(j))
                for j in range(1, NX)
            ]

        def _recv(self):
            for copy in self.copies:
                copy.wait_recv()

        def step2(self):
            self._recv()
            w, h = self.w, self.half
            a = w.at[y, z, pl.ds(0, h), pl.ds(LANE, HC - LANE)]
            b = w.at[y, z, pl.ds(h, h), pl.ds(LANE, HC - LANE)]
            self.copies = [rcopy(a, a, z_peer(j)) for j in range(1, NZ)]
            self.copies += [rcopy(b, b, y_peer(j)) for j in range(1, NY)]

        def step3(self):
            self._recv()
            w, h = self.w, self.half
            rest = pl.ds(LANE, HC - LANE)
            self.rings = [
                (lambda yy, part: w.at[yy, part, pl.ds(0, h), rest], y, NY, y_peer, NZ),
                (lambda zz, part: w.at[part, zz, pl.ds(h, h), rest], z, NZ, z_peer, NY),
            ]
            self.copies = []
            for place, me, size, peer, across in self.rings:
                mine = place(me, pl.ds(0, across))
                self.copies.append([
                    rcopy(mine, mine, peer(j)) for j in sorted({1, size - 1})
                ])

        def step4(self):
            sent, self.copies = self.copies, []
            for (place, me, size, peer, across), ring in zip(self.rings, sent):
                if size == 2:
                    self.copies += ring
                    continue
                part = across // 2
                for copy, j, first in ((ring[0], 1, 0), (ring[1], size - 1, part)):
                    copy.wait_recv()
                    passed = place((me + size - j) % size, pl.ds(first, part))
                    self.copies.append(rcopy(passed, passed, peer(j)))

        def wait(self):
            self._recv()

    class Scatter:
        def __init__(self, g, bufs, over_x=False):
            self.g = g
            self.ra, self.rb, self.sa, self.sbb, self.ra2, self.rb2, self.s2, self.r3 = bufs[:8]
            self.main = self.s2.shape[0]
            self.over_x = over_x
            if over_x:
                self.rx1, self.sx, self.rx2, self.sx2, self.rx3 = bufs[8:]
            half, rows = HC // 2, pl.ds(0, self.main)
            self.rings = (
                (lambda d, part: (part, (z + d) % NZ, rows, pl.ds(0, half)),
                 self.ra, NZ, z_peer, NY),
                (lambda d, part: ((y + d) % NY, part, rows, pl.ds(half, half)),
                 self.rb, NY, y_peer, NZ),
            )

        def step1(self):
            self.relay, self.full = [], []
            for index, land, size, peer, across in self.rings:
                part = across // 2
                lo, hi = pl.ds(0, part), pl.ds(part, part)
                if size == 2:
                    continue
                self.relay.append([
                    rcopy(self.g.at[index(2, lo)], land.at[1, lo], peer(1)),
                    rcopy(self.g.at[index(2, hi)], land.at[1, hi], peer(3)),
                ])

        def step1b(self):
            for index, land, size, peer, across in self.rings:
                part = across // 2
                lo, hi = pl.ds(0, part), pl.ds(part, part)
                if size == 2:
                    every = pl.ds(0, across)
                    self.full.append([rcopy(self.g.at[index(1, every)], land.at[0], peer(1))])
                else:
                    self.full.append([
                        rcopy(self.g.at[index(1, hi)], land.at[0, hi], peer(1)),
                        rcopy(self.g.at[index(3, lo)], land.at[2, lo], peer(3)),
                    ])

        def x_step1(self):
            part = pl.ds(self.main, self.g.shape[2] - self.main)
            self.xs = [
                rcopy(self.g.at[:, :, part, pl.ds(j * LANE, LANE)], self.rx1.at[j - 1], x_peer(j))
                for j in range(1, NX)
            ]

        def step1c(self):
            for (index, land, size, peer, across), relay, full in zip(
                self.rings, self.relay, self.full
            ):
                part = across // 2
                for copy, j, here in (
                    (relay[0], 1, pl.ds(0, part)), (relay[1], 3, pl.ds(part, part))
                ):
                    copy.wait_recv()
                    at = index(j, here)
                    self.g[at] = (
                        self.g[at].astype(F32) + land[1, here].astype(F32)
                    ).astype(BF)
                    full.append(rcopy(self.g.at[at], land.at[j - 1, here], peer(j)))

        def step2(self):
            g, half, m = self.g, HC // 2, self.main
            for copy in self.full[0]:
                copy.wait_recv()
            for yy in range(NY):
                total = g[yy, z, 0:m, 0:half].astype(F32)
                for j in sorted({1, NZ - 1}):
                    total = total + self.ra[j - 1, yy].astype(F32)
                self.sa[yy] = total.astype(BF)
            self.a = [
                rcopy(self.sa.at[(y + j) % NY], self.ra2.at[j - 1], y_peer(j))
                for j in range(1, NY)
            ]
            for copy in self.full[1]:
                copy.wait_recv()
            for zz in range(NZ):
                total = g[y, zz, 0:m, half:HC].astype(F32)
                for j in sorted({1, NY - 1}):
                    total = total + self.rb[j - 1, zz].astype(F32)
                self.sbb[zz] = total.astype(BF)
            self.b = [
                rcopy(self.sbb.at[(z + j) % NZ], self.rb2.at[j - 1], z_peer(j))
                for j in range(1, NZ)
            ]

        def x_step2(self):
            for copy in self.xs:
                copy.wait_recv()
            for yy in range(NY):
                total = self.g[yy, :, self.main:, 0:LANE].astype(F32)
                for j in range(1, NX):
                    total = total + self.rx1[j - 1, yy].astype(F32)
                self.sx[yy] = total.astype(BF)
            self.xs = [
                rcopy(self.sx.at[:, (z + j) % NZ], self.rx2.at[j - 1], z_peer(j))
                for j in range(1, NZ)
            ]

        def x_step3(self):
            for copy in self.xs:
                copy.wait_recv()
            total = self.sx[:, z].astype(F32)
            for j in range(1, NZ):
                total = total + self.rx2[j - 1].astype(F32)
            self.sx2[...] = total.astype(BF)
            self.xs = [
                rcopy(self.sx2.at[(y + j) % NY], self.rx3.at[j - 1], y_peer(j))
                for j in range(1, NY)
            ]

        def x_finish(self):
            for copy in self.xs:
                copy.wait_recv()
            total = self.sx2[y].astype(F32)
            for j in range(1, NY):
                total = total + self.rx3[j - 1].astype(F32)
            return total

        def step3(self):
            half = HC // 2
            for copy in self.a:
                copy.wait_recv()
            total = self.sa[y].astype(F32)
            for j in range(1, NY):
                total = total + self.ra2[j - 1].astype(F32)
            self.s2[:, 0:half] = total.astype(BF)
            for copy in self.b:
                copy.wait_recv()
            total = self.sbb[z].astype(F32)
            for j in range(1, NZ):
                total = total + self.rb2[j - 1].astype(F32)
            self.s2[:, half:HC] = total.astype(BF)
            self.x = [
                rcopy(self.s2.at[:, pl.ds(j * LANE, LANE)], self.r3.at[j - 1], x_peer(j))
                for j in range(1, NX)
            ]

        def finish(self):
            for copy in self.x:
                copy.wait_recv()
            total = self.s2[:, 0:LANE].astype(F32)
            for j in range(1, NX):
                total = total + self.r3[j - 1].astype(F32)
            return total

    def local(a, b, i):
        copy = pltpu.make_async_copy(a, b, lsem.at[i])
        copy.start()
        return copy

    barrier = pltpu.get_barrier_semaphore()
    partners = [x_peer(j) for j in range(1, NX)] + [sib] + [n_peer(j) for j in range(1, NN)]
    for device in partners:
        pl.semaphore_signal(barrier, inc=1, device_id=device, device_id_type=pl.DeviceIdType.MESH)
    get_lat, get_weo, get_wno, get_weh, get_wnh, get_ea, get_nct, get_ect = [
        local(a, b, i)
        for i, (a, b) in enumerate((
            (lat_hbm, lat), (weo_hbm, weo), (wno_hbm, wno),
            (weh, w_eh.at[:, :, :, pl.ds(0, LANE)]), (wnh, w_nh.at[:, :, :, pl.ds(0, LANE)]),
            (ea_hbm, ea), (nct_hbm, nct), (ect_hbm, ect),
        ))
    ]

    srcf = src[...].reshape(1, E).astype(F32)
    dstf = dst[...].reshape(1, E).astype(F32)
    is_far = srcf >= float(N)
    slotf = jnp.where(is_far, jnp.floor((srcf - float(N)) * (1.0 / LANE)), -1.0)
    blocks = E // LANE
    for b in range(blocks):
        piece = slice(b * LANE, (b + 1) * LANE)
        src_b[piece, :] = jnp.broadcast_to(srcf[:, piece], (LANE, LANE)).T
        dst_b[piece, :] = jnp.broadcast_to(dstf[:, piece], (LANE, LANE)).T
    src_col = src_b[...]
    slot_col = jnp.where(
        src_col >= float(N), jnp.floor((src_col - float(N)) * (1.0 / LANE)), -1.0
    )
    order = sublane_iota(E)
    place = sublane_iota(NN * PER)
    for b in range(blocks):
        piece = slice(b * LANE, (b + 1) * LANE)
        mine = jnp.broadcast_to(slotf[:, piece], (E, LANE))
        before = (slot_col == mine) & (order < lane_iota(E) + float(b * LANE))
        rank = jnp.sum(jnp.where(before, 1.0, 0.0), axis=0, keepdims=True)
        q = jnp.where(is_far[:, piece], slotf[:, piece] * float(SLOT) + rank, -1.0)
        pt[:, piece] = one_hot(place == jnp.broadcast_to(q, (NN * PER, LANE)))
        q_b[piece, :] = jnp.broadcast_to(q, (LANE, LANE)).T
    row_in_block = (src_col - LANE * jnp.floor(src_col * (1.0 / LANE))).astype(BF)
    wanted = mm(pt[...], row_in_block).astype(BF)
    for p in range(NN):
        rq_out[p] = wanted[p * PER:(p + 1) * PER]
    get_weo.wait()
    get_wno.wait()
    w_eo[:, :, :, 0:LANE] = weo[...].T.reshape(NY, NZ, L // NN, LANE)
    w_no[:, :, :, 0:LANE] = wno[...].T.reshape(NY, NZ, L // NN, LANE)
    pl.semaphore_wait(barrier, len(partners))

    gat_eh, gat_nh, gat_no, gat_eo = Gather(w_eh), Gather(w_nh), Gather(w_no), Gather(w_eo)
    gat_eh.step1(weh.at[y, z])
    ask = [
        rcopy(rq_out.at[(n + j) % NN], rq_in.at[n], n_peer(j)) for j in range(1, NN)
    ]
    rq_in[n] = rq_out[n]
    get_lat.wait()
    get_ea.wait()
    rows_ea = ToRows(lambda g: ei.at[2, g]).send_all(lambda xx: ea.at[pl.ds(xx * RE, RE), :])
    gat_eo.step1(w_eo.at[y, z, :, pl.ds(0, LANE)])
    gat_nh.step1(wnh.at[y, z])
    gat_no.step1(w_no.at[y, z, :, pl.ds(0, LANE)])

    rows_dst = ToRows(lambda g: ei.at[1, g])
    for j in [*far_first, 0]:
        xx = at_x(j)
        pick = select_lanes(dst_b[pl.ds(xx * RE, RE), :], N)
        dstc[xx] = mm(pick, lat[...]).astype(BF)
        rows_dst.send(j, dstc.at[xx])

    gat_eh.step2()

    for copy in ask:
        copy.wait_recv()
    half_rows = sublane_iota(PER) < float(SLOT)
    for d in range(NN):
        base = jnp.where(
            half_rows,
            (sb[0, d] * LANE).astype(F32),
            (sb[1, d] * LANE).astype(F32),
        )
        rsel[d] = select_lanes(rq_in[d].astype(F32) + base, N)
    given = mm(rsel[...].reshape(NN * PER, N), lat[...]).astype(BF)
    for d in range(NN):
        row_out[d] = given[d * PER:(d + 1) * PER]
    halo = [
        rcopy(row_out.at[(n + j) % NN], row_in.at[n], n_peer(j)) for j in range(1, NN)
    ]
    row_in[n] = row_out[n]

    gat_eo.step2()
    gat_eh.step3()
    rows_ea.forward()
    rows_dst.forward()

    nodes_down = sublane_iota(N)
    for b in range(blocks):
        piece = slice(b * LANE, (b + 1) * LANE)
        dt[:, piece] = one_hot(nodes_down == jnp.broadcast_to(dstf[:, piece], (N, LANE)))
        slt[:, piece] = one_hot(nodes_down == jnp.broadcast_to(srcf[:, piece], (N, LANE)))

    gat_eo.step3()
    gat_eh.step4()

    for copy in halo:
        copy.wait_recv()
    table = jnp.concatenate([lat[...], row_in[...].reshape(NN * PER, LANE)], axis=0)
    rows_src = ToRows(lambda g: ei.at[0, g])
    for j in [*far_first, 0]:
        xx = at_x(j)
        here = pl.ds(xx * RE, RE)
        pick = jnp.concatenate(
            [select_lanes(src_b[here, :], N), select_lanes(q_b[here, :], NN * PER)], axis=1
        )
        srcc[xx] = mm(pick, table).astype(BF)
        rows_src.send(j, srcc.at[xx])
    gat_eo.step4()

    get_weh.wait()
    gat_eh.wait()
    rows_ea.wait()
    rows_dst.wait()
    weh_all = w_eh[...].reshape(3 * L, HC)
    hpre[...] = mm(wide(ei, (1,)), weh_all[L:2 * L]) + mm(wide(ei, (2,)), weh_all[2 * L:])
    gat_nh.step2()
    gat_no.step2()
    rows_src.forward()
    get_nct.wait()
    rows_lat = ToRows(lambda g: ni.at[0, g]).send_all(lambda xx: lat.at[pl.ds(xx * RN, RN), :])
    rows_cot = ToRows(lambda g: cot.at[g]).send_all(lambda xx: nct.at[pl.ds(xx * RN, RN), :])
    rows_src.wait()
    pre = hpre[...] + mm(wide(ei, (0,)), weh_all[:L])
    hpre[...] = pre
    hidden[...] = (pre * jax.nn.sigmoid(pre)).astype(BF)
    gat_nh.step3()
    gat_no.step3()
    gat_eo.wait()
    weo_all = w_eo[...].reshape(L, HC)
    chan_m = ToChan(mm_nt(hidden[...], weo_all), pb_m, rx_m, ch_m)
    chan_m.forward()
    gat_nh.step4()
    gat_no.step4()
    rows_lat.forward()
    rows_cot.forward()
    chan_m.wait()

    fresh = (ea[...].astype(F32) + ch_m[...].reshape(E, LANE).astype(F32)).astype(BF)
    nsum[...] = mm(dt[...], fresh).astype(BF).reshape(NX, RN, LANE)
    rows_sum = ToRows(lambda g: ni.at[1, g]).send_all(lambda xx: nsum.at[xx])

    rows_lat.wait()
    rows_cot.wait()
    get_wnh.wait()
    gat_nh.wait()
    gat_no.wait()
    wnh_all = w_nh[...].reshape(2 * L, HC)
    cots = wide(cot)
    npre[...] = mm(wide(ni, (0,)), wnh_all[:L])
    pulled = mm(cots, w_no[...].reshape(L, HC))
    rows_sum.forward()
    rows_sum.wait()
    pre = npre[...] + mm(wide(ni, (1,)), wnh_all[L:])
    sig = jax.nn.sigmoid(pre)
    node_hidden = (pre * sig).astype(BF)
    node_back = (pulled * (sig * (1.0 + pre * (1.0 - sig)))).astype(BF)
    chan_n1 = ToChan(mm_nt(node_back, wnh_all[L:]), pb_n.at[1], rx_n.at[1], ch_n.at[1])
    chan_n0 = ToChan(mm_nt(node_back, wnh_all[:L]), pb_n.at[0], rx_n.at[0], ch_n.at[0])
    chan_n1.forward()
    chan_n0.forward()

    def weight_grad(g, values, back):
        per_y = g.shape[1] * g.shape[2]
        for yy in range(NY):
            part = mm_tn(values[:, yy * per_y:(yy + 1) * per_y], back)
            g[yy] = part.astype(BF).reshape(g.shape[1:])

    sc_eh, sc_eo = Scatter(g_eh, rs_bufs[0:13], True), Scatter(g_eo, rs_bufs[13:21])
    sc_nh, sc_no = Scatter(g_nh, rs_bufs[21:29]), Scatter(g_no, rs_bufs[29:37])
    weight_grad(g_nh, jnp.concatenate([wide(ni, (0,)), wide(ni, (1,))], axis=1), node_back)
    sc_nh.step1()
    weight_grad(g_no, cots, node_hidden)
    sc_no.step1()
    sc_nh.step1b()
    sc_no.step1b()

    chan_n1.wait()
    share = ch_n[1].reshape(N, LANE)
    get_ect.wait()
    rows_mg = ToRows(lambda g: mg.at[g])
    for j in [*far_first, 0]:
        xx = at_x(j)
        here = pl.ds(xx * RE, RE)
        total = ect[here, :].astype(F32) + mm(select_lanes(dst_b[here, :], N), share)
        ge[here, :] = total
        mgc[xx] = total.astype(BF)
        rows_mg.send(j, mgc.at[xx])
    pre = hpre[...]
    sig = jax.nn.sigmoid(pre)
    hpre[...] = sig * (1.0 + pre * (1.0 - sig))
    rows_mg.forward()
    sc_nh.step1c()
    sc_no.step1c()
    rows_mg.wait()
    message_grad = wide(mg)
    edge_back = (mm(message_grad, weo_all) * hpre[...]).astype(BF)
    def pull(t):
        return ToChan(
            mm_nt(edge_back, weh_all[t * L:(t + 1) * L]), pb_e.at[t], rx_e.at[t], ch_e.at[t]
        )

    chan_e = [pull(0)]
    weight_grad(
        g_eh, jnp.concatenate([wide(ei, (t,)) for t in range(3)], axis=1), edge_back
    )
    sc_eh.step1()
    chan_e[0].forward()
    sc_eh.step1b()
    chan_e += [pull(1), pull(2)]
    chan_e[1].forward()
    weight_grad(g_eo, message_grad, hidden[...])
    sc_eo.step1()
    chan_e[2].forward()
    sc_eo.step1b()
    sc_eh.x_step1()
    sc_nh.step2()
    sc_no.step2()

    chan_e[0].wait()
    from_source = ch_e[0].reshape(E, LANE)
    back = mm(pt[...], from_source).astype(BF)
    for p in range(NN):
        ret_out[p] = back[p * PER:(p + 1) * PER]
    returned = [
        rcopy(ret_out.at[(n + j) % NN], ret_in.at[n], n_peer(j)) for j in range(1, NN)
    ]
    ret_in[n] = ret_out[n]
    sc_eh.step1c()
    sc_eo.step1c()
    sc_nh.step3()
    sc_no.step3()
    chan_n0.wait()
    chan_e[1].wait()
    gl[...] = (
        nct[...].astype(F32)
        + ch_n[0].reshape(N, LANE).astype(F32)
        + mm(slt[...], from_source)
        + mm(dt[...], ch_e[1].reshape(E, LANE))
    )
    chan_e[2].wait()
    ge[...] = ge[...] + ch_e[2].reshape(E, LANE).astype(F32)
    put_ge = local(ge, ge_hbm, 8)
    for copy in returned:
        copy.wait_recv()
    gl[...] = gl[...] + mm_tn(
        rsel[...].reshape(NN * PER, N), ret_in[...].reshape(NN * PER, LANE)
    )
    put_gl = local(gl, gl_hbm, 9)
    out_nh[...] = node_scale * sc_nh.finish()
    out_no[...] = node_scale * sc_no.finish()
    sc_eh.step2()
    sc_eo.step2()
    sc_eh.x_step2()
    sc_eh.step3()
    sc_eo.step3()
    sc_eh.x_step3()
    out_eh[:sc_eh.main, :] = edge_scale * sc_eh.finish()
    out_eo[...] = edge_scale * sc_eo.finish()
    out_eh[sc_eh.main:, :] = edge_scale * sc_eh.x_finish()
    put_ge.wait()
    put_gl.wait()
    flush()


def hand_over(*refs):
    count = (len(refs) - 2) // 3
    given, taken, held = refs[:count], refs[count:2 * count], refs[2 * count:3 * count]
    in_sem, out_sem = refs[3 * count:]
    loads = [
        pltpu.make_async_copy(a, b, in_sem.at[i]) for i, (a, b) in enumerate(zip(given, held))
    ]
    stores = [
        pltpu.make_async_copy(a, b, out_sem.at[i]) for i, (a, b) in enumerate(zip(held, taken))
    ]
    for load in loads:
        load.start()
    for load, store in zip(loads, stores):
        load.wait()
        store.start()
    for store in stores:
        store.wait()


def on_device(
    dims,
    latents, edge_attr, edge_src, edge_dst, send_blocks,
    edge_hidden_w, edge_out_w, node_hidden_w, node_out_w,
    node_cotangent, edge_cotangent,
):
    NX, NY, NZ = dims
    NN = NY * NZ
    E, N = edge_attr.shape[0], latents.shape[0]
    RE, RN = E // NX, N // NX
    G = NX * NC
    L, HC = G * LANE, NX * LANE
    PER = E // 2 // NN

    def v(*shape, dtype=BF):
        return pltpu.VMEM(shape, dtype)

    chunks = [3 * L // NN, 2 * L // NN, L // NN, L // NN]
    rs = []
    for i in (0, 3, 1, 2):
        part = max(16, chunks[i] // 6 // 16 * 16) if i == 0 else 0
        ch = chunks[i] - part
        rs += [
            v(NZ - 1, NY, ch, HC // 2), v(NY - 1, NZ, ch, HC // 2),
            v(NY, ch, HC // 2), v(NZ, ch, HC // 2),
            v(NY - 1, ch, HC // 2), v(NZ - 1, ch, HC // 2),
            v(ch, HC), v(NX - 1, ch, LANE),
        ]
        if part:
            rs += [
                v(NX - 1, NY, NZ, part, LANE), v(NY, NZ, part, LANE),
                v(NZ - 1, NY, part, LANE), v(NY, part, LANE), v(NY - 1, part, LANE),
            ]
    scratch = [
        pltpu.SemaphoreType.DMA((320,)), pltpu.SemaphoreType.DMA((320,)),
        pltpu.SemaphoreType.DMA((10,)),
        v(N, LANE), v(E, LANE), v(LANE, L), v(LANE, L), v(N, LANE), v(E, LANE),
        v(N, LANE, dtype=F32), v(E, LANE, dtype=F32),
        v(3, G, RE, LANE), v(2, G, RN, LANE), v(G, RN, LANE), v(G, RE, LANE),
        v(RE, HC), v(RE, HC, dtype=F32), v(RN, HC, dtype=F32),
        v(E, LANE, dtype=F32), v(E, LANE, dtype=F32), v(E, LANE, dtype=F32),
        v(N, E), v(N, E), v(NN * PER, E), v(NN, PER, N),
        *[v(NN, PER, LANE) for _ in range(6)],
        v(NX, RE, LANE), v(NX, RE, LANE), v(NX, RN, LANE), v(NX, RE, LANE),
        *[v(NY, NZ, ch, HC) for ch in chunks],
        *[v(NY, NZ, ch, HC) for ch in chunks],
        v(NX, NC, RE, LANE), v(NX, RE, LANE), v(NX, RE, LANE),
        v(2, NX, NC, RN, LANE), v(2, NX, RN, LANE), v(2, NX, RN, LANE),
        v(3, NX, NC, RE, LANE), v(3, NX, RE, LANE), v(3, NX, RE, LANE),
        *rs,
    ]
    vmem = pl.BlockSpec(memory_space=pltpu.VMEM)
    smem = pl.BlockSpec(memory_space=pltpu.SMEM)
    hbm = pl.BlockSpec(memory_space=pl.ANY)

    def f(*shape):
        return jax.ShapeDtypeStruct(shape, F32)

    results = pl.pallas_call(
        functools.partial(kernel, dims),
        out_shape=(
            f(N, LANE), f(E, LANE), f(chunks[0], LANE), f(chunks[3], LANE),
            f(chunks[1], LANE), f(chunks[2], LANE),
        ),
        in_specs=[hbm, hbm, vmem, vmem, smem] + [hbm] * 6,
        out_specs=[hbm, hbm] + [vmem] * 4,
        scratch_shapes=scratch,
        compiler_params=pltpu.CompilerParams(
            collective_id=0, has_side_effects=True, vmem_limit_bytes=64 * 1024 * 1024 - 65536
        ),
    )(
        latents, edge_attr, edge_src, edge_dst, send_blocks[0].T,
        edge_hidden_w.reshape(NY, NZ, chunks[0], LANE), edge_out_w,
        node_hidden_w.reshape(NY, NZ, chunks[1], LANE), node_out_w,
        node_cotangent, edge_cotangent,
    )
    gl, ge, g_eh, g_eo, g_nh, g_no = pl.pallas_call(
        hand_over,
        out_shape=tuple(jax.ShapeDtypeStruct(r.shape, r.dtype) for r in results),
        in_specs=[hbm] * 6,
        out_specs=[hbm] * 6,
        scratch_shapes=[
            *[pltpu.VMEM(r.shape, r.dtype) for r in results],
            pltpu.SemaphoreType.DMA((6,)), pltpu.SemaphoreType.DMA((6,)),
        ],
        compiler_params=pltpu.CompilerParams(vmem_limit_bytes=60 * 1024 * 1024),
    )(*results)
    return gl, ge, g_eh, g_eo.T, g_nh, g_no.T


def solution(mesh):
    nodes, chans = mesh.shape["node"], mesh.shape["chan"]
    nz = 1
    while nz * nz < nodes:
        nz *= 2
    dims = (chans // NC, nodes // nz, nz)
    return jax.shard_map(
        functools.partial(on_device, dims),
        mesh=mesh,
        in_specs=(
            P("node", "chan"),
            P("node", "chan"),
            P("node"),
            P("node"),
            P("node", None, None),
            P(None, "chan"),
            P("chan", None),
            P(None, "chan"),
            P("chan", None),
            P("node", "chan"),
            P("node", "chan"),
        ),
        out_specs=(
            P("node", "chan"),
            P("node", "chan"),
            P("node", "chan"),
            P("chan", "node"),
            P("node", "chan"),
            P("chan", "node"),
        ),
        check_vma=False,
    )
```

```python
import functools

import jax
import jax.numpy as jnp
from jax import lax
from jax.experimental import pallas as pl
from jax.experimental.pallas import tpu as pltpu
from jax.sharding import PartitionSpec as P

BF = jnp.bfloat16
F32 = jnp.float32
LANE = 128
NC = 2


def mm(a, b):
    return jnp.dot(a, b, preferred_element_type=F32)


def mm_nt(a, b):
    return lax.dot_general(a, b, (((1,), (1,)), ((), ())), preferred_element_type=F32)


def mm_tn(a, b):
    return lax.dot_general(a, b, (((0,), (0,)), ((), ())), preferred_element_type=F32)


def one_hot(mask):
    return jnp.where(mask, 1.0, 0.0).astype(BF)


def lane_iota(rows):
    return lax.broadcasted_iota(jnp.int32, (rows, LANE), 1).astype(F32)


def sublane_iota(rows):
    return lax.broadcasted_iota(jnp.int32, (rows, LANE), 0).astype(F32)


def select_lanes(index, width):
    lanes = lane_iota(index.shape[0])
    return jnp.concatenate(
        [one_hot(index == lanes + float(b * LANE)) for b in range(width // LANE)], axis=1
    )


def wide(ref, lead=()):
    groups = ref.shape[len(lead)]
    return jnp.concatenate([ref[(*lead, g)] for g in range(groups)], axis=1)


def kernel(
    dims,
    lat_hbm, ea_hbm, src, dst, sb, weh, weo_hbm, wnh, wno_hbm, nct_hbm, ect_hbm,
    gl_hbm, ge_hbm, out_eh, out_eo, out_nh, out_no,
    ssem, rsem, lsem,
    lat, ea, weo, wno, nct, ect, gl, ge,
    ei, ni, cot, mg, hidden, hpre, npre,
    src_b, dst_b, q_b, dt, slt, pt, rsel,
    rq_out, rq_in, row_out, row_in, ret_out, ret_in,
    srcc, dstc, nsum, mgc,
    w_eh, w_nh, w_no, w_eo,
    g_eh, g_nh, g_no, g_eo,
    pb_m, rx_m, ch_m, pb_n, rx_n, ch_n, pb_e, rx_e, ch_e,
    *rs_bufs,
):
    NX, NY, NZ = dims
    NN = NY * NZ
    E, N = ea.shape[0], lat.shape[0]
    RE, RN = E // NX, N // NX
    L = NX * NC * LANE
    HC = NX * LANE
    PER = E // 2 // NN
    SLOT = PER // 2
    edge_scale = float(E * NN) ** (-0.5)
    node_scale = float(N * NN) ** (-0.5)

    n, k = lax.axis_index("node"), lax.axis_index("chan")
    x, c = k // NC, k % NC
    y, z = n // NZ, n % NZ

    def at_x(j):
        return (x + j) % NX

    def x_peer(j):
        return (n, at_x(j) * NC + c)

    def y_peer(j):
        return (((y + j) % NY) * NZ + z, k)

    def z_peer(j):
        return (y * NZ + (z + j) % NZ, k)

    def n_peer(j):
        return ((n + j) % NN, k)

    sib = (n, x * NC + 1 - c)

    pending = []
    used = [0]

    def rcopy(a, b, device):
        i = used[0]
        used[0] += 1
        copy = pltpu.make_async_remote_copy(
            src_ref=a, dst_ref=b, send_sem=ssem.at[i], recv_sem=rsem.at[i],
            device_id=device, device_id_type=pl.DeviceIdType.MESH,
        )
        copy.start()
        pending.append(copy)
        return copy

    def flush():
        while pending:
            pending.pop(0).wait_send()

    far_first = sorted(range(1, NX), key=lambda j: -min(j, NX - j))

    class ToRows:
        def __init__(self, put):
            self.put, self.near, self.far = put, [], []

        def send(self, j, chunk):
            if j:
                self.far.append((j, rcopy(chunk, self.put(x * NC + c), x_peer(j))))
            else:
                self.put(x * NC + c)[...] = chunk[...]
                self.near.append(rcopy(chunk, self.put(x * NC + c), sib))
            return self

        def send_all(self, chunk):
            for j in [*far_first, 0]:
                self.send(j, chunk(at_x(j)))
            return self

        def forward(self):
            for j, copy in self.far:
                copy.wait_recv()
                slot = self.put(at_x(NX - j) * NC + c)
                self.near.append(rcopy(slot, slot, sib))

        def wait(self):
            for copy in self.near:
                copy.wait_recv()

    class ToChan:
        def __init__(self, value, pb, rx, ch):
            self.pb, self.rx, self.ch, self.far = pb, rx, ch, []
            for g in range(NX * NC):
                pb[g // NC, g % NC] = value[:, g * LANE:(g + 1) * LANE].astype(BF)
            self.near = [
                (j, rcopy(pb.at[at_x(j), 1 - c], rx.at[at_x(j)], sib)) for j in [*far_first, 0]
            ]

        def forward(self):
            for j, copy in self.near:
                copy.wait_recv()
                xx = at_x(j)
                total = (self.rx[xx].astype(F32) + self.pb[xx, c].astype(F32)).astype(BF)
                if j:
                    self.rx[xx] = total
                    self.far.append(rcopy(self.rx.at[xx], self.ch.at[x], x_peer(j)))
                else:
                    self.ch[x] = total

        def wait(self):
            for copy in self.far:
                copy.wait_recv()

    class Gather:
        def __init__(self, w):
            self.w, self.half = w, w.shape[2] // 2

        def step1(self, own):
            w = self.w
            self.copies = [
                rcopy(own, w.at[y, z, :, pl.ds((NX - j) * LANE, LANE)], x_peer(j))
                for j in range(1, NX)
            ]

        def _recv(self):
            for copy in self.copies:
                copy.wait_recv()

        def step2(self):
            self._recv()
            w, h = self.w, self.half
            a = w.at[y, z, pl.ds(0, h), pl.ds(LANE, HC - LANE)]
            b = w.at[y, z, pl.ds(h, h), pl.ds(LANE, HC - LANE)]
            self.copies = [rcopy(a, a, z_peer(j)) for j in range(1, NZ)]
            self.copies += [rcopy(b, b, y_peer(j)) for j in range(1, NY)]

        def step3(self):
            self._recv()
            w, h = self.w, self.half
            rest = pl.ds(LANE, HC - LANE)
            self.rings = [
                (lambda yy, part: w.at[yy, part, pl.ds(0, h), rest], y, NY, y_peer, NZ),
                (lambda zz, part: w.at[part, zz, pl.ds(h, h), rest], z, NZ, z_peer, NY),
            ]
            self.copies = []
            for place, me, size, peer, across in self.rings:
                mine = place(me, pl.ds(0, across))
                self.copies.append([
                    rcopy(mine, mine, peer(j)) for j in sorted({1, size - 1})
                ])

        def step4(self):
            sent, self.copies = self.copies, []
            for (place, me, size, peer, across), ring in zip(self.rings, sent):
                if size == 2:
                    self.copies += ring
                    continue
                part = across // 2
                for copy, j, first in ((ring[0], 1, 0), (ring[1], size - 1, part)):
                    copy.wait_recv()
                    passed = place((me + size - j) % size, pl.ds(first, part))
                    self.copies.append(rcopy(passed, passed, peer(j)))

        def wait(self):
            self._recv()

    class Scatter:
        def __init__(self, g, bufs, over_x=False):
            self.g = g
            self.ra, self.rb, self.sa, self.sbb, self.ra2, self.rb2, self.s2, self.r3 = bufs[:8]
            self.main = self.s2.shape[0]
            self.over_x = over_x
            if over_x:
                self.rx1, self.sx, self.rx2, self.sx2, self.rx3 = bufs[8:]
            half, rows = HC // 2, pl.ds(0, self.main)
            self.rings = (
                (lambda d, part: (part, (z + d) % NZ, rows, pl.ds(0, half)),
                 self.ra, NZ, z_peer, NY),
                (lambda d, part: ((y + d) % NY, part, rows, pl.ds(half, half)),
                 self.rb, NY, y_peer, NZ),
            )

        def step1(self):
            self.relay, self.full = [], []
            for index, land, size, peer, across in self.rings:
                part = across // 2
                lo, hi = pl.ds(0, part), pl.ds(part, part)
                if size == 2:
                    continue
                self.relay.append([
                    rcopy(self.g.at[index(2, lo)], land.at[1, lo], peer(1)),
                    rcopy(self.g.at[index(2, hi)], land.at[1, hi], peer(3)),
                ])

        def step1b(self):
            for index, land, size, peer, across in self.rings:
                part = across // 2
                lo, hi = pl.ds(0, part), pl.ds(part, part)
                if size == 2:
                    every = pl.ds(0, across)
                    self.full.append([rcopy(self.g.at[index(1, every)], land.at[0], peer(1))])
                else:
                    self.full.append([
                        rcopy(self.g.at[index(1, hi)], land.at[0, hi], peer(1)),
                        rcopy(self.g.at[index(3, lo)], land.at[2, lo], peer(3)),
                    ])

        def x_step1(self):
            part = pl.ds(self.main, self.g.shape[2] - self.main)
            self.xs = [
                rcopy(self.g.at[:, :, part, pl.ds(j * LANE, LANE)], self.rx1.at[j - 1], x_peer(j))
                for j in range(1, NX)
            ]

        def step1c(self):
            for (index, land, size, peer, across), relay, full in zip(
                self.rings, self.relay, self.full
            ):
                part = across // 2
                for copy, j, here in (
                    (relay[0], 1, pl.ds(0, part)), (relay[1], 3, pl.ds(part, part))
                ):
                    copy.wait_recv()
                    at = index(j, here)
                    self.g[at] = (
                        self.g[at].astype(F32) + land[1, here].astype(F32)
                    ).astype(BF)
                    full.append(rcopy(self.g.at[at], land.at[j - 1, here], peer(j)))

        def step2(self):
            g, half, m = self.g, HC // 2, self.main
            for copy in self.full[0]:
                copy.wait_recv()
            for yy in range(NY):
                total = g[yy, z, 0:m, 0:half].astype(F32)
                for j in sorted({1, NZ - 1}):
                    total = total + self.ra[j - 1, yy].astype(F32)
                self.sa[yy] = total.astype(BF)
            self.a = [
                rcopy(self.sa.at[(y + j) % NY], self.ra2.at[j - 1], y_peer(j))
                for j in range(1, NY)
            ]
            for copy in self.full[1]:
                copy.wait_recv()
            for zz in range(NZ):
                total = g[y, zz, 0:m, half:HC].astype(F32)
                for j in sorted({1, NY - 1}):
                    total = total + self.rb[j - 1, zz].astype(F32)
                self.sbb[zz] = total.astype(BF)
            self.b = [
                rcopy(self.sbb.at[(z + j) % NZ], self.rb2.at[j - 1], z_peer(j))
                for j in range(1, NZ)
            ]

        def x_step2(self):
            for copy in self.xs:
                copy.wait_recv()
            for yy in range(NY):
                total = self.g[yy, :, self.main:, 0:LANE].astype(F32)
                for j in range(1, NX):
                    total = total + self.rx1[j - 1, yy].astype(F32)
                self.sx[yy] = total.astype(BF)
            self.xs = [
                rcopy(self.sx.at[:, (z + j) % NZ], self.rx2.at[j - 1], z_peer(j))
                for j in range(1, NZ)
            ]

        def x_step3(self):
            for copy in self.xs:
                copy.wait_recv()
            total = self.sx[:, z].astype(F32)
            for j in range(1, NZ):
                total = total + self.rx2[j - 1].astype(F32)
            self.sx2[...] = total.astype(BF)
            self.xs = [
                rcopy(self.sx2.at[(y + j) % NY], self.rx3.at[j - 1], y_peer(j))
                for j in range(1, NY)
            ]

        def x_finish(self):
            for copy in self.xs:
                copy.wait_recv()
            total = self.sx2[y].astype(F32)
            for j in range(1, NY):
                total = total + self.rx3[j - 1].astype(F32)
            return total

        def step3(self):
            half = HC // 2
            for copy in self.a:
                copy.wait_recv()
            total = self.sa[y].astype(F32)
            for j in range(1, NY):
                total = total + self.ra2[j - 1].astype(F32)
            self.s2[:, 0:half] = total.astype(BF)
            for copy in self.b:
                copy.wait_recv()
            total = self.sbb[z].astype(F32)
            for j in range(1, NZ):
                total = total + self.rb2[j - 1].astype(F32)
            self.s2[:, half:HC] = total.astype(BF)
            self.x = [
                rcopy(self.s2.at[:, pl.ds(j * LANE, LANE)], self.r3.at[j - 1], x_peer(j))
                for j in range(1, NX)
            ]

        def finish(self):
            for copy in self.x:
                copy.wait_recv()
            total = self.s2[:, 0:LANE].astype(F32)
            for j in range(1, NX):
                total = total + self.r3[j - 1].astype(F32)
            return total

    def local(a, b, i):
        copy = pltpu.make_async_copy(a, b, lsem.at[i])
        copy.start()
        return copy

    barrier = pltpu.get_barrier_semaphore()
    partners = [x_peer(j) for j in range(1, NX)] + [sib] + [n_peer(j) for j in range(1, NN)]
    for device in partners:
        pl.semaphore_signal(barrier, inc=1, device_id=device, device_id_type=pl.DeviceIdType.MESH)
    get_lat, get_weo, get_wno, get_weh, get_wnh, get_ea, get_nct, get_ect = [
        local(a, b, i)
        for i, (a, b) in enumerate((
            (lat_hbm, lat), (weo_hbm, weo), (wno_hbm, wno),
            (weh, w_eh.at[:, :, :, pl.ds(0, LANE)]), (wnh, w_nh.at[:, :, :, pl.ds(0, LANE)]),
            (ea_hbm, ea), (nct_hbm, nct), (ect_hbm, ect),
        ))
    ]

    srcf = src[...].reshape(1, E).astype(F32)
    dstf = dst[...].reshape(1, E).astype(F32)
    is_far = srcf >= float(N)
    slotf = jnp.where(is_far, jnp.floor((srcf - float(N)) * (1.0 / LANE)), -1.0)
    blocks = E // LANE
    for b in range(blocks):
        piece = slice(b * LANE, (b + 1) * LANE)
        src_b[piece, :] = jnp.broadcast_to(srcf[:, piece], (LANE, LANE)).T
        dst_b[piece, :] = jnp.broadcast_to(dstf[:, piece], (LANE, LANE)).T
    src_col = src_b[...]
    slot_col = jnp.where(
        src_col >= float(N), jnp.floor((src_col - float(N)) * (1.0 / LANE)), -1.0
    )
    order = sublane_iota(E)
    place = sublane_iota(NN * PER)
    for b in range(blocks):
        piece = slice(b * LANE, (b + 1) * LANE)
        mine = jnp.broadcast_to(slotf[:, piece], (E, LANE))
        before = (slot_col == mine) & (order < lane_iota(E) + float(b * LANE))
        rank = jnp.sum(jnp.where(before, 1.0, 0.0), axis=0, keepdims=True)
        q = jnp.where(is_far[:, piece], slotf[:, piece] * float(SLOT) + rank, -1.0)
        pt[:, piece] = one_hot(place == jnp.broadcast_to(q, (NN * PER, LANE)))
        q_b[piece, :] = jnp.broadcast_to(q, (LANE, LANE)).T
    row_in_block = (src_col - LANE * jnp.floor(src_col * (1.0 / LANE))).astype(BF)
    wanted = mm(pt[...], row_in_block).astype(BF)
    for p in range(NN):
        rq_out[p] = wanted[p * PER:(p + 1) * PER]
    get_weo.wait()
    get_wno.wait()
    w_eo[:, :, :, 0:LANE] = weo[...].T.reshape(NY, NZ, L // NN, LANE)
    w_no[:, :, :, 0:LANE] = wno[...].T.reshape(NY, NZ, L // NN, LANE)
    pl.semaphore_wait(barrier, len(partners))

    gat_eh, gat_nh, gat_no, gat_eo = Gather(w_eh), Gather(w_nh), Gather(w_no), Gather(w_eo)
    gat_eh.step1(weh.at[y, z])
    gat_eo.step1(w_eo.at[y, z, :, pl.ds(0, LANE)])
    gat_nh.step1(wnh.at[y, z])
    gat_no.step1(w_no.at[y, z, :, pl.ds(0, LANE)])
    ask = [
        rcopy(rq_out.at[(n + j) % NN], rq_in.at[n], n_peer(j)) for j in range(1, NN)
    ]
    rq_in[n] = rq_out[n]
    get_lat.wait()
    get_ea.wait()
    rows_ea = ToRows(lambda g: ei.at[2, g]).send_all(lambda xx: ea.at[pl.ds(xx * RE, RE), :])

    rows_dst = ToRows(lambda g: ei.at[1, g])
    for j in [*far_first, 0]:
        xx = at_x(j)
        pick = select_lanes(dst_b[pl.ds(xx * RE, RE), :], N)
        dstc[xx] = mm(pick, lat[...]).astype(BF)
        rows_dst.send(j, dstc.at[xx])

    gat_eh.step2()

    for copy in ask:
        copy.wait_recv()
    half_rows = sublane_iota(PER) < float(SLOT)
    for d in range(NN):
        base = jnp.where(
            half_rows,
            (sb[0, d] * LANE).astype(F32),
            (sb[1, d] * LANE).astype(F32),
        )
        rsel[d] = select_lanes(rq_in[d].astype(F32) + base, N)
    given = mm(rsel[...].reshape(NN * PER, N), lat[...]).astype(BF)
    for d in range(NN):
        row_out[d] = given[d * PER:(d + 1) * PER]
    halo = [
        rcopy(row_out.at[(n + j) % NN], row_in.at[n], n_peer(j)) for j in range(1, NN)
    ]
    row_in[n] = row_out[n]

    gat_eo.step2()
    gat_eh.step3()
    rows_ea.forward()
    rows_dst.forward()

    nodes_down = sublane_iota(N)
    for b in range(blocks):
        piece = slice(b * LANE, (b + 1) * LANE)
        dt[:, piece] = one_hot(nodes_down == jnp.broadcast_to(dstf[:, piece], (N, LANE)))
        slt[:, piece] = one_hot(nodes_down == jnp.broadcast_to(srcf[:, piece], (N, LANE)))

    gat_eo.step3()
    gat_eh.step4()

    for copy in halo:
        copy.wait_recv()
    table = jnp.concatenate([lat[...], row_in[...].reshape(NN * PER, LANE)], axis=0)
    rows_src = ToRows(lambda g: ei.at[0, g])
    for j in [*far_first, 0]:
        xx = at_x(j)
        here = pl.ds(xx * RE, RE)
        pick = jnp.concatenate(
            [select_lanes(src_b[here, :], N), select_lanes(q_b[here, :], NN * PER)], axis=1
        )
        srcc[xx] = mm(pick, table).astype(BF)
        rows_src.send(j, srcc.at[xx])
    gat_eo.step4()

    get_weh.wait()
    gat_eh.wait()
    rows_ea.wait()
    rows_dst.wait()
    weh_all = w_eh[...].reshape(3 * L, HC)
    hpre[...] = mm(wide(ei, (1,)), weh_all[L:2 * L]) + mm(wide(ei, (2,)), weh_all[2 * L:])
    gat_nh.step2()
    gat_no.step2()
    rows_src.forward()
    get_nct.wait()
    rows_lat = ToRows(lambda g: ni.at[0, g]).send_all(lambda xx: lat.at[pl.ds(xx * RN, RN), :])
    rows_cot = ToRows(lambda g: cot.at[g]).send_all(lambda xx: nct.at[pl.ds(xx * RN, RN), :])
    rows_src.wait()
    pre = hpre[...] + mm(wide(ei, (0,)), weh_all[:L])
    hpre[...] = pre
    hidden[...] = (pre * jax.nn.sigmoid(pre)).astype(BF)
    gat_nh.step3()
    gat_no.step3()
    gat_eo.wait()
    weo_all = w_eo[...].reshape(L, HC)
    chan_m = ToChan(mm_nt(hidden[...], weo_all), pb_m, rx_m, ch_m)
    chan_m.forward()
    gat_nh.step4()
    gat_no.step4()
    rows_lat.forward()
    rows_cot.forward()
    chan_m.wait()

    fresh = (ea[...].astype(F32) + ch_m[...].reshape(E, LANE).astype(F32)).astype(BF)
    nsum[...] = mm(dt[...], fresh).astype(BF).reshape(NX, RN, LANE)
    rows_sum = ToRows(lambda g: ni.at[1, g]).send_all(lambda xx: nsum.at[xx])

    rows_lat.wait()
    rows_cot.wait()
    get_wnh.wait()
    gat_nh.wait()
    gat_no.wait()
    wnh_all = w_nh[...].reshape(2 * L, HC)
    cots = wide(cot)
    npre[...] = mm(wide(ni, (0,)), wnh_all[:L])
    pulled = mm(cots, w_no[...].reshape(L, HC))
    rows_sum.forward()
    rows_sum.wait()
    pre = npre[...] + mm(wide(ni, (1,)), wnh_all[L:])
    sig = jax.nn.sigmoid(pre)
    node_hidden = (pre * sig).astype(BF)
    node_back = (pulled * (sig * (1.0 + pre * (1.0 - sig)))).astype(BF)
    chan_n1 = ToChan(mm_nt(node_back, wnh_all[L:]), pb_n.at[1], rx_n.at[1], ch_n.at[1])
    chan_n0 = ToChan(mm_nt(node_back, wnh_all[:L]), pb_n.at[0], rx_n.at[0], ch_n.at[0])
    chan_n1.forward()
    chan_n0.forward()

    def weight_grad(g, values, back):
        per_y = g.shape[1] * g.shape[2]
        for yy in range(NY):
            part = mm_tn(values[:, yy * per_y:(yy + 1) * per_y], back)
            g[yy] = part.astype(BF).reshape(g.shape[1:])

    sc_eh, sc_eo = Scatter(g_eh, rs_bufs[0:13], True), Scatter(g_eo, rs_bufs[13:21])
    sc_nh, sc_no = Scatter(g_nh, rs_bufs[21:29]), Scatter(g_no, rs_bufs[29:37])
    weight_grad(g_nh, jnp.concatenate([wide(ni, (0,)), wide(ni, (1,))], axis=1), node_back)
    sc_nh.step1()
    weight_grad(g_no, cots, node_hidden)
    sc_no.step1()
    sc_nh.step1b()
    sc_no.step1b()

    chan_n1.wait()
    share = ch_n[1].reshape(N, LANE)
    get_ect.wait()
    rows_mg = ToRows(lambda g: mg.at[g])
    for j in [*far_first, 0]:
        xx = at_x(j)
        here = pl.ds(xx * RE, RE)
        total = ect[here, :].astype(F32) + mm(select_lanes(dst_b[here, :], N), share)
        ge[here, :] = total
        mgc[xx] = total.astype(BF)
        rows_mg.send(j, mgc.at[xx])
    pre = hpre[...]
    sig = jax.nn.sigmoid(pre)
    hpre[...] = sig * (1.0 + pre * (1.0 - sig))
    rows_mg.forward()
    sc_nh.step1c()
    sc_no.step1c()
    rows_mg.wait()
    message_grad = wide(mg)
    edge_back = (mm(message_grad, weo_all) * hpre[...]).astype(BF)
    def pull(t):
        return ToChan(
            mm_nt(edge_back, weh_all[t * L:(t + 1) * L]), pb_e.at[t], rx_e.at[t], ch_e.at[t]
        )

    chan_e = [pull(0)]
    weight_grad(
        g_eh, jnp.concatenate([wide(ei, (t,)) for t in range(3)], axis=1), edge_back
    )
    sc_eh.step1()
    chan_e[0].forward()
    sc_eh.step1b()
    chan_e += [pull(1), pull(2)]
    chan_e[1].forward()
    weight_grad(g_eo, message_grad, hidden[...])
    sc_eo.step1()
    chan_e[2].forward()
    sc_eo.step1b()
    sc_eh.x_step1()
    sc_nh.step2()
    sc_no.step2()

    chan_e[0].wait()
    from_source = ch_e[0].reshape(E, LANE)
    back = mm(pt[...], from_source).astype(BF)
    for p in range(NN):
        ret_out[p] = back[p * PER:(p + 1) * PER]
    returned = [
        rcopy(ret_out.at[(n + j) % NN], ret_in.at[n], n_peer(j)) for j in range(1, NN)
    ]
    ret_in[n] = ret_out[n]
    sc_eh.step1c()
    sc_eo.step1c()
    sc_nh.step3()
    sc_no.step3()
    chan_n0.wait()
    chan_e[1].wait()
    gl[...] = (
        nct[...].astype(F32)
        + ch_n[0].reshape(N, LANE).astype(F32)
        + mm(slt[...], from_source)
        + mm(dt[...], ch_e[1].reshape(E, LANE))
    )
    chan_e[2].wait()
    ge[...] = ge[...] + ch_e[2].reshape(E, LANE).astype(F32)
    put_ge = local(ge, ge_hbm, 8)
    for copy in returned:
        copy.wait_recv()
    gl[...] = gl[...] + mm_tn(
        rsel[...].reshape(NN * PER, N), ret_in[...].reshape(NN * PER, LANE)
    )
    put_gl = local(gl, gl_hbm, 9)
    out_nh[...] = node_scale * sc_nh.finish()
    out_no[...] = node_scale * sc_no.finish()
    sc_eh.step2()
    sc_eo.step2()
    sc_eh.x_step2()
    sc_eh.step3()
    sc_eo.step3()
    sc_eh.x_step3()
    out_eh[:sc_eh.main, :] = edge_scale * sc_eh.finish()
    out_eo[...] = edge_scale * sc_eo.finish()
    out_eh[sc_eh.main:, :] = edge_scale * sc_eh.x_finish()
    put_ge.wait()
    put_gl.wait()
    flush()


def hand_over(*refs):
    count = (len(refs) - 2) // 3
    given, taken, held = refs[:count], refs[count:2 * count], refs[2 * count:3 * count]
    in_sem, out_sem = refs[3 * count:]
    loads = [
        pltpu.make_async_copy(a, b, in_sem.at[i]) for i, (a, b) in enumerate(zip(given, held))
    ]
    stores = [
        pltpu.make_async_copy(a, b, out_sem.at[i]) for i, (a, b) in enumerate(zip(held, taken))
    ]
    for load in loads:
        load.start()
    for load, store in zip(loads, stores):
        load.wait()
        store.start()
    for store in stores:
        store.wait()


def on_device(
    dims,
    latents, edge_attr, edge_src, edge_dst, send_blocks,
    edge_hidden_w, edge_out_w, node_hidden_w, node_out_w,
    node_cotangent, edge_cotangent,
):
    NX, NY, NZ = dims
    NN = NY * NZ
    E, N = edge_attr.shape[0], latents.shape[0]
    RE, RN = E // NX, N // NX
    G = NX * NC
    L, HC = G * LANE, NX * LANE
    PER = E // 2 // NN

    def v(*shape, dtype=BF):
        return pltpu.VMEM(shape, dtype)

    chunks = [3 * L // NN, 2 * L // NN, L // NN, L // NN]
    rs = []
    for i in (0, 3, 1, 2):
        part = max(16, chunks[i] // 6 // 16 * 16) if i == 0 else 0
        ch = chunks[i] - part
        rs += [
            v(NZ - 1, NY, ch, HC // 2), v(NY - 1, NZ, ch, HC // 2),
            v(NY, ch, HC // 2), v(NZ, ch, HC // 2),
            v(NY - 1, ch, HC // 2), v(NZ - 1, ch, HC // 2),
            v(ch, HC), v(NX - 1, ch, LANE),
        ]
        if part:
            rs += [
                v(NX - 1, NY, NZ, part, LANE), v(NY, NZ, part, LANE),
                v(NZ - 1, NY, part, LANE), v(NY, part, LANE), v(NY - 1, part, LANE),
            ]
    scratch = [
        pltpu.SemaphoreType.DMA((320,)), pltpu.SemaphoreType.DMA((320,)),
        pltpu.SemaphoreType.DMA((10,)),
        v(N, LANE), v(E, LANE), v(LANE, L), v(LANE, L), v(N, LANE), v(E, LANE),
        v(N, LANE, dtype=F32), v(E, LANE, dtype=F32),
        v(3, G, RE, LANE), v(2, G, RN, LANE), v(G, RN, LANE), v(G, RE, LANE),
        v(RE, HC), v(RE, HC, dtype=F32), v(RN, HC, dtype=F32),
        v(E, LANE, dtype=F32), v(E, LANE, dtype=F32), v(E, LANE, dtype=F32),
        v(N, E), v(N, E), v(NN * PER, E), v(NN, PER, N),
        *[v(NN, PER, LANE) for _ in range(6)],
        v(NX, RE, LANE), v(NX, RE, LANE), v(NX, RN, LANE), v(NX, RE, LANE),
        *[v(NY, NZ, ch, HC) for ch in chunks],
        *[v(NY, NZ, ch, HC) for ch in chunks],
        v(NX, NC, RE, LANE), v(NX, RE, LANE), v(NX, RE, LANE),
        v(2, NX, NC, RN, LANE), v(2, NX, RN, LANE), v(2, NX, RN, LANE),
        v(3, NX, NC, RE, LANE), v(3, NX, RE, LANE), v(3, NX, RE, LANE),
        *rs,
    ]
    vmem = pl.BlockSpec(memory_space=pltpu.VMEM)
    smem = pl.BlockSpec(memory_space=pltpu.SMEM)
    hbm = pl.BlockSpec(memory_space=pl.ANY)

    def f(*shape):
        return jax.ShapeDtypeStruct(shape, F32)

    results = pl.pallas_call(
        functools.partial(kernel, dims),
        out_shape=(
            f(N, LANE), f(E, LANE), f(chunks[0], LANE), f(chunks[3], LANE),
            f(chunks[1], LANE), f(chunks[2], LANE),
        ),
        in_specs=[hbm, hbm, vmem, vmem, smem] + [hbm] * 6,
        out_specs=[hbm, hbm] + [vmem] * 4,
        scratch_shapes=scratch,
        compiler_params=pltpu.CompilerParams(
            collective_id=0, has_side_effects=True, vmem_limit_bytes=64 * 1024 * 1024 - 65536
        ),
    )(
        latents, edge_attr, edge_src, edge_dst, send_blocks[0].T,
        edge_hidden_w.reshape(NY, NZ, chunks[0], LANE), edge_out_w,
        node_hidden_w.reshape(NY, NZ, chunks[1], LANE), node_out_w,
        node_cotangent, edge_cotangent,
    )
    gl, ge, g_eh, g_eo, g_nh, g_no = pl.pallas_call(
        hand_over,
        out_shape=tuple(jax.ShapeDtypeStruct(r.shape, r.dtype) for r in results),
        in_specs=[hbm] * 6,
        out_specs=[hbm] * 6,
        scratch_shapes=[
            *[pltpu.VMEM(r.shape, r.dtype) for r in results],
            pltpu.SemaphoreType.DMA((6,)), pltpu.SemaphoreType.DMA((6,)),
        ],
        compiler_params=pltpu.CompilerParams(vmem_limit_bytes=60 * 1024 * 1024),
    )(*results)
    return gl, ge, g_eh, g_eo.T, g_nh, g_no.T


def solution(mesh):
    nodes, chans = mesh.shape["node"], mesh.shape["chan"]
    nz = 1
    while nz * nz < nodes:
        nz *= 2
    dims = (chans // NC, nodes // nz, nz)
    return jax.shard_map(
        functools.partial(on_device, dims),
        mesh=mesh,
        in_specs=(
            P("node", "chan"),
            P("node", "chan"),
            P("node"),
            P("node"),
            P("node", None, None),
            P(None, "chan"),
            P("chan", None),
            P(None, "chan"),
            P("chan", None),
            P("node", "chan"),
            P("node", "chan"),
        ),
        out_specs=(
            P("node", "chan"),
            P("node", "chan"),
            P("node", "chan"),
            P("chan", "node"),
            P("node", "chan"),
            P("chan", "node"),
        ),
        check_vma=False,
    )
```

```python
import functools

import jax
import jax.numpy as jnp
from jax import lax
from jax.experimental import pallas as pl
from jax.experimental.pallas import tpu as pltpu
from jax.sharding import PartitionSpec as P

BF = jnp.bfloat16
F32 = jnp.float32
LANE = 128
NC = 2


def mm(a, b):
    return jnp.dot(a, b, preferred_element_type=F32)


def mm_nt(a, b):
    return lax.dot_general(a, b, (((1,), (1,)), ((), ())), preferred_element_type=F32)


def mm_tn(a, b):
    return lax.dot_general(a, b, (((0,), (0,)), ((), ())), preferred_element_type=F32)


def one_hot(mask):
    return jnp.where(mask, 1.0, 0.0).astype(BF)


def lane_iota(rows):
    return lax.broadcasted_iota(jnp.int32, (rows, LANE), 1).astype(F32)


def sublane_iota(rows):
    return lax.broadcasted_iota(jnp.int32, (rows, LANE), 0).astype(F32)


def select_lanes(index, width):
    lanes = lane_iota(index.shape[0])
    return jnp.concatenate(
        [one_hot(index == lanes + float(b * LANE)) for b in range(width // LANE)], axis=1
    )


def wide(ref, lead=()):
    groups = ref.shape[len(lead)]
    return jnp.concatenate([ref[(*lead, g)] for g in range(groups)], axis=1)


def kernel(
    dims,
    lat_hbm, ea_hbm, src, dst, sb, weh, weo_hbm, wnh, wno_hbm, nct_hbm, ect_hbm,
    gl_hbm, ge_hbm, out_eh, out_eo, out_nh, out_no,
    ssem, rsem, lsem,
    lat, ea, weo, wno, nct, ect, gl, ge,
    ei, ni, cot, mg, hidden, hpre, npre,
    src_b, dst_b, q_b, dt, slt, pt, rsel,
    rq_out, rq_in, row_out, row_in, ret_out, ret_in,
    srcc, dstc, nsum, mgc,
    w_eh, w_nh, w_no, w_eo,
    g_eh, g_nh, g_no, g_eo,
    pb_m, rx_m, ch_m, pb_n, rx_n, ch_n, pb_e, rx_e, ch_e,
    *rs_bufs,
):
    NX, NY, NZ = dims
    NN = NY * NZ
    E, N = ea.shape[0], lat.shape[0]
    RE, RN = E // NX, N // NX
    L = NX * NC * LANE
    HC = NX * LANE
    PER = E // 2 // NN
    SLOT = PER // 2
    edge_scale = float(E * NN) ** (-0.5)
    node_scale = float(N * NN) ** (-0.5)

    n, k = lax.axis_index("node"), lax.axis_index("chan")
    x, c = k // NC, k % NC
    y, z = n // NZ, n % NZ

    def at_x(j):
        return (x + j) % NX

    def x_peer(j):
        return (n, at_x(j) * NC + c)

    def y_peer(j):
        return (((y + j) % NY) * NZ + z, k)

    def z_peer(j):
        return (y * NZ + (z + j) % NZ, k)

    def n_peer(j):
        return ((n + j) % NN, k)

    sib = (n, x * NC + 1 - c)

    pending = []
    used = [0]

    def rcopy(a, b, device):
        i = used[0]
        used[0] += 1
        copy = pltpu.make_async_remote_copy(
            src_ref=a, dst_ref=b, send_sem=ssem.at[i], recv_sem=rsem.at[i],
            device_id=device, device_id_type=pl.DeviceIdType.MESH,
        )
        copy.start()
        pending.append(copy)
        return copy

    def flush(count):
        for _ in range(count):
            pending.pop(0).wait_send()

    far_first = sorted(range(1, NX), key=lambda j: -min(j, NX - j))

    class ToRows:
        def __init__(self, put):
            self.put, self.near, self.far = put, [], []

        def send(self, j, chunk):
            if j:
                self.far.append((j, rcopy(chunk, self.put(x * NC + c), x_peer(j))))
            else:
                self.put(x * NC + c)[...] = chunk[...]
                self.near.append(rcopy(chunk, self.put(x * NC + c), sib))
            return self

        def send_all(self, chunk):
            for j in [*far_first, 0]:
                self.send(j, chunk(at_x(j)))
            return self

        def forward(self):
            for j, copy in self.far:
                copy.wait_recv()
                slot = self.put(at_x(NX - j) * NC + c)
                self.near.append(rcopy(slot, slot, sib))

        def wait(self):
            for copy in self.near:
                copy.wait_recv()

    class ToChan:
        def __init__(self, value, pb, rx, ch):
            self.pb, self.rx, self.ch, self.far = pb, rx, ch, []
            for g in range(NX * NC):
                pb[g // NC, g % NC] = value[:, g * LANE:(g + 1) * LANE].astype(BF)
            self.near = [
                (j, rcopy(pb.at[at_x(j), 1 - c], rx.at[at_x(j)], sib)) for j in [*far_first, 0]
            ]

        def forward(self):
            for j, copy in self.near:
                copy.wait_recv()
                xx = at_x(j)
                total = (self.rx[xx].astype(F32) + self.pb[xx, c].astype(F32)).astype(BF)
                if j:
                    self.rx[xx] = total
                    self.far.append(rcopy(self.rx.at[xx], self.ch.at[x], x_peer(j)))
                else:
                    self.ch[x] = total

        def wait(self):
            for copy in self.far:
                copy.wait_recv()

    class Gather:
        def __init__(self, w):
            self.w, self.half = w, w.shape[2] // 2

        def step1(self, own):
            w = self.w
            self.copies = [
                rcopy(own, w.at[y, z, :, pl.ds((NX - j) * LANE, LANE)], x_peer(j))
                for j in range(1, NX)
            ]

        def _recv(self):
            for copy in self.copies:
                copy.wait_recv()

        def step2(self):
            self._recv()
            w, h = self.w, self.half
            a = w.at[y, z, pl.ds(0, h), pl.ds(LANE, HC - LANE)]
            b = w.at[y, z, pl.ds(h, h), pl.ds(LANE, HC - LANE)]
            self.copies = [rcopy(a, a, z_peer(j)) for j in range(1, NZ)]
            self.copies += [rcopy(b, b, y_peer(j)) for j in range(1, NY)]

        def step3(self):
            self._recv()
            w, h = self.w, self.half
            rest = pl.ds(LANE, HC - LANE)
            self.rings = [
                (lambda yy, part: w.at[yy, part, pl.ds(0, h), rest], y, NY, y_peer, NZ),
                (lambda zz, part: w.at[part, zz, pl.ds(h, h), rest], z, NZ, z_peer, NY),
            ]
            self.copies = []
            for place, me, size, peer, across in self.rings:
                mine = place(me, pl.ds(0, across))
                self.copies.append([
                    rcopy(mine, mine, peer(j)) for j in sorted({1, size - 1})
                ])

        def step4(self):
            sent, self.copies = self.copies, []
            for (place, me, size, peer, across), ring in zip(self.rings, sent):
                if size == 2:
                    self.copies += ring
                    continue
                part = across // 2
                for copy, j, first in ((ring[0], 1, 0), (ring[1], size - 1, part)):
                    copy.wait_recv()
                    passed = place((me + size - j) % size, pl.ds(first, part))
                    self.copies.append(rcopy(passed, passed, peer(j)))

        def wait(self):
            self._recv()

    class Scatter:
        def __init__(self, g, bufs, over_x=False):
            self.g = g
            self.ra, self.rb, self.sa, self.sbb, self.ra2, self.rb2, self.s2, self.r3 = bufs[:8]
            self.main = self.s2.shape[0]
            self.over_x = over_x
            if over_x:
                self.rx1, self.sx, self.rx2, self.sx2, self.rx3 = bufs[8:]
            half, rows = HC // 2, pl.ds(0, self.main)
            self.rings = (
                (lambda d, part: (part, (z + d) % NZ, rows, pl.ds(0, half)),
                 self.ra, NZ, z_peer, NY),
                (lambda d, part: ((y + d) % NY, part, rows, pl.ds(half, half)),
                 self.rb, NY, y_peer, NZ),
            )

        def step1(self):
            self.relay, self.full = [], []
            for index, land, size, peer, across in self.rings:
                part = across // 2
                lo, hi = pl.ds(0, part), pl.ds(part, part)
                if size == 2:
                    continue
                self.relay.append([
                    rcopy(self.g.at[index(2, lo)], land.at[1, lo], peer(1)),
                    rcopy(self.g.at[index(2, hi)], land.at[1, hi], peer(3)),
                ])

        def step1b(self):
            for index, land, size, peer, across in self.rings:
                part = across // 2
                lo, hi = pl.ds(0, part), pl.ds(part, part)
                if size == 2:
                    every = pl.ds(0, across)
                    self.full.append([rcopy(self.g.at[index(1, every)], land.at[0], peer(1))])
                else:
                    self.full.append([
                        rcopy(self.g.at[index(1, hi)], land.at[0, hi], peer(1)),
                        rcopy(self.g.at[index(3, lo)], land.at[2, lo], peer(3)),
                    ])

        def x_step1(self):
            part = pl.ds(self.main, self.g.shape[2] - self.main)
            self.xs = [
                rcopy(self.g.at[:, :, part, pl.ds(j * LANE, LANE)], self.rx1.at[j - 1], x_peer(j))
                for j in range(1, NX)
            ]

        def step1c(self):
            for (index, land, size, peer, across), relay, full in zip(
                self.rings, self.relay, self.full
            ):
                part = across // 2
                for copy, j, here in (
                    (relay[0], 1, pl.ds(0, part)), (relay[1], 3, pl.ds(part, part))
                ):
                    copy.wait_recv()
                    at = index(j, here)
                    self.g[at] = (
                        self.g[at].astype(F32) + land[1, here].astype(F32)
                    ).astype(BF)
                    full.append(rcopy(self.g.at[at], land.at[j - 1, here], peer(j)))

        def step2(self):
            g, half, m = self.g, HC // 2, self.main
            for copy in self.full[0]:
                copy.wait_recv()
            for yy in range(NY):
                total = g[yy, z, 0:m, 0:half].astype(F32)
                for j in sorted({1, NZ - 1}):
                    total = total + self.ra[j - 1, yy].astype(F32)
                self.sa[yy] = total.astype(BF)
            self.a = [
                rcopy(self.sa.at[(y + j) % NY], self.ra2.at[j - 1], y_peer(j))
                for j in range(1, NY)
            ]
            for copy in self.full[1]:
                copy.wait_recv()
            for zz in range(NZ):
                total = g[y, zz, 0:m, half:HC].astype(F32)
                for j in sorted({1, NY - 1}):
                    total = total + self.rb[j - 1, zz].astype(F32)
                self.sbb[zz] = total.astype(BF)
            self.b = [
                rcopy(self.sbb.at[(z + j) % NZ], self.rb2.at[j - 1], z_peer(j))
                for j in range(1, NZ)
            ]

        def x_step2(self):
            for copy in self.xs:
                copy.wait_recv()
            for yy in range(NY):
                total = self.g[yy, :, self.main:, 0:LANE].astype(F32)
                for j in range(1, NX):
                    total = total + self.rx1[j - 1, yy].astype(F32)
                self.sx[yy] = total.astype(BF)
            self.xs = [
                rcopy(self.sx.at[:, (z + j) % NZ], self.rx2.at[j - 1], z_peer(j))
                for j in range(1, NZ)
            ]

        def x_step3(self):
            for copy in self.xs:
                copy.wait_recv()
            total = self.sx[:, z].astype(F32)
            for j in range(1, NZ):
                total = total + self.rx2[j - 1].astype(F32)
            self.sx2[...] = total.astype(BF)
            self.xs = [
                rcopy(self.sx2.at[(y + j) % NY], self.rx3.at[j - 1], y_peer(j))
                for j in range(1, NY)
            ]

        def x_finish(self):
            for copy in self.xs:
                copy.wait_recv()
            total = self.sx2[y].astype(F32)
            for j in range(1, NY):
                total = total + self.rx3[j - 1].astype(F32)
            return total

        def step3(self):
            half = HC // 2
            for copy in self.a:
                copy.wait_recv()
            total = self.sa[y].astype(F32)
            for j in range(1, NY):
                total = total + self.ra2[j - 1].astype(F32)
            self.s2[:, 0:half] = total.astype(BF)
            for copy in self.b:
                copy.wait_recv()
            total = self.sbb[z].astype(F32)
            for j in range(1, NZ):
                total = total + self.rb2[j - 1].astype(F32)
            self.s2[:, half:HC] = total.astype(BF)
            self.x = [
                rcopy(self.s2.at[:, pl.ds(j * LANE, LANE)], self.r3.at[j - 1], x_peer(j))
                for j in range(1, NX)
            ]

        def finish(self):
            for copy in self.x:
                copy.wait_recv()
            total = self.s2[:, 0:LANE].astype(F32)
            for j in range(1, NX):
                total = total + self.r3[j - 1].astype(F32)
            return total

    def local(a, b, i):
        copy = pltpu.make_async_copy(a, b, lsem.at[i])
        copy.start()
        return copy

    barrier = pltpu.get_barrier_semaphore()
    partners = [x_peer(j) for j in range(1, NX)] + [sib] + [n_peer(j) for j in range(1, NN)]
    for device in partners:
        pl.semaphore_signal(barrier, inc=1, device_id=device, device_id_type=pl.DeviceIdType.MESH)
    get_lat, get_weo, get_wno, get_weh, get_wnh, get_ea, get_nct, get_ect = [
        local(a, b, i)
        for i, (a, b) in enumerate((
            (lat_hbm, lat), (weo_hbm, weo), (wno_hbm, wno),
            (weh, w_eh.at[:, :, :, pl.ds(0, LANE)]), (wnh, w_nh.at[:, :, :, pl.ds(0, LANE)]),
            (ea_hbm, ea), (nct_hbm, nct), (ect_hbm, ect),
        ))
    ]

    srcf = src[...].reshape(1, E).astype(F32)
    dstf = dst[...].reshape(1, E).astype(F32)
    is_far = srcf >= float(N)
    slotf = jnp.where(is_far, jnp.floor((srcf - float(N)) * (1.0 / LANE)), -1.0)
    blocks = E // LANE
    for b in range(blocks):
        piece = slice(b * LANE, (b + 1) * LANE)
        src_b[piece, :] = jnp.broadcast_to(srcf[:, piece], (LANE, LANE)).T
        dst_b[piece, :] = jnp.broadcast_to(dstf[:, piece], (LANE, LANE)).T
    src_col = src_b[...]
    slot_col = jnp.where(
        src_col >= float(N), jnp.floor((src_col - float(N)) * (1.0 / LANE)), -1.0
    )
    order = sublane_iota(E)
    place = sublane_iota(NN * PER)
    for b in range(blocks):
        piece = slice(b * LANE, (b + 1) * LANE)
        mine = jnp.broadcast_to(slotf[:, piece], (E, LANE))
        before = (slot_col == mine) & (order < lane_iota(E) + float(b * LANE))
        rank = jnp.sum(jnp.where(before, 1.0, 0.0), axis=0, keepdims=True)
        q = jnp.where(is_far[:, piece], slotf[:, piece] * float(SLOT) + rank, -1.0)
        pt[:, piece] = one_hot(place == jnp.broadcast_to(q, (NN * PER, LANE)))
        q_b[piece, :] = jnp.broadcast_to(q, (LANE, LANE)).T
    row_in_block = (src_col - LANE * jnp.floor(src_col * (1.0 / LANE))).astype(BF)
    wanted = mm(pt[...], row_in_block).astype(BF)
    for p in range(NN):
        rq_out[p] = wanted[p * PER:(p + 1) * PER]
    get_weo.wait()
    get_wno.wait()
    w_eo[:, :, :, 0:LANE] = weo[...].T.reshape(NY, NZ, L // NN, LANE)
    w_no[:, :, :, 0:LANE] = wno[...].T.reshape(NY, NZ, L // NN, LANE)
    pl.semaphore_wait(barrier, len(partners))

    gat_eh, gat_nh, gat_no, gat_eo = Gather(w_eh), Gather(w_nh), Gather(w_no), Gather(w_eo)
    gat_eh.step1(weh.at[y, z])
    gat_eo.step1(w_eo.at[y, z, :, pl.ds(0, LANE)])
    gat_nh.step1(wnh.at[y, z])
    gat_no.step1(w_no.at[y, z, :, pl.ds(0, LANE)])
    ask = [
        rcopy(rq_out.at[(n + j) % NN], rq_in.at[n], n_peer(j)) for j in range(1, NN)
    ]
    rq_in[n] = rq_out[n]
    get_lat.wait()
    get_ea.wait()
    rows_ea = ToRows(lambda g: ei.at[2, g]).send_all(lambda xx: ea.at[pl.ds(xx * RE, RE), :])

    rows_dst = ToRows(lambda g: ei.at[1, g])
    for j in [*far_first, 0]:
        xx = at_x(j)
        pick = select_lanes(dst_b[pl.ds(xx * RE, RE), :], N)
        dstc[xx] = mm(pick, lat[...]).astype(BF)
        rows_dst.send(j, dstc.at[xx])

    gat_eh.step2()
    gat_eo.step2()

    for copy in ask:
        copy.wait_recv()
    half_rows = sublane_iota(PER) < float(SLOT)
    for d in range(NN):
        base = jnp.where(
            half_rows,
            (sb[0, d] * LANE).astype(F32),
            (sb[1, d] * LANE).astype(F32),
        )
        rsel[d] = select_lanes(rq_in[d].astype(F32) + base, N)
    given = mm(rsel[...].reshape(NN * PER, N), lat[...]).astype(BF)
    for d in range(NN):
        row_out[d] = given[d * PER:(d + 1) * PER]
    halo = [
        rcopy(row_out.at[(n + j) % NN], row_in.at[n], n_peer(j)) for j in range(1, NN)
    ]
    row_in[n] = row_out[n]

    gat_eh.step3()
    rows_ea.forward()
    rows_dst.forward()

    nodes_down = sublane_iota(N)
    for b in range(blocks):
        piece = slice(b * LANE, (b + 1) * LANE)
        dt[:, piece] = one_hot(nodes_down == jnp.broadcast_to(dstf[:, piece], (N, LANE)))
        slt[:, piece] = one_hot(nodes_down == jnp.broadcast_to(srcf[:, piece], (N, LANE)))

    gat_eo.step3()
    gat_eh.step4()

    for copy in halo:
        copy.wait_recv()
    table = jnp.concatenate([lat[...], row_in[...].reshape(NN * PER, LANE)], axis=0)
    rows_src = ToRows(lambda g: ei.at[0, g])
    for j in [*far_first, 0]:
        xx = at_x(j)
        here = pl.ds(xx * RE, RE)
        pick = jnp.concatenate(
            [select_lanes(src_b[here, :], N), select_lanes(q_b[here, :], NN * PER)], axis=1
        )
        srcc[xx] = mm(pick, table).astype(BF)
        rows_src.send(j, srcc.at[xx])
    gat_eo.step4()

    get_weh.wait()
    gat_eh.wait()
    rows_ea.wait()
    rows_dst.wait()
    weh_all = w_eh[...].reshape(3 * L, HC)
    hpre[...] = mm(wide(ei, (1,)), weh_all[L:2 * L]) + mm(wide(ei, (2,)), weh_all[2 * L:])
    gat_nh.step2()
    gat_no.step2()
    rows_src.forward()
    get_nct.wait()
    rows_lat = ToRows(lambda g: ni.at[0, g]).send_all(lambda xx: lat.at[pl.ds(xx * RN, RN), :])
    rows_cot = ToRows(lambda g: cot.at[g]).send_all(lambda xx: nct.at[pl.ds(xx * RN, RN), :])
    rows_src.wait()
    pre = hpre[...] + mm(wide(ei, (0,)), weh_all[:L])
    hpre[...] = pre
    hidden[...] = (pre * jax.nn.sigmoid(pre)).astype(BF)
    gat_nh.step3()
    gat_no.step3()
    gat_eo.wait()
    weo_all = w_eo[...].reshape(L, HC)
    chan_m = ToChan(mm_nt(hidden[...], weo_all), pb_m, rx_m, ch_m)
    chan_m.forward()
    gat_nh.step4()
    gat_no.step4()
    rows_lat.forward()
    rows_cot.forward()
    chan_m.wait()

    fresh = (ea[...].astype(F32) + ch_m[...].reshape(E, LANE).astype(F32)).astype(BF)
    nsum[...] = mm(dt[...], fresh).astype(BF).reshape(NX, RN, LANE)
    rows_sum = ToRows(lambda g: ni.at[1, g]).send_all(lambda xx: nsum.at[xx])

    rows_lat.wait()
    rows_cot.wait()
    get_wnh.wait()
    gat_nh.wait()
    gat_no.wait()
    wnh_all = w_nh[...].reshape(2 * L, HC)
    cots = wide(cot)
    npre[...] = mm(wide(ni, (0,)), wnh_all[:L])
    pulled = mm(cots, w_no[...].reshape(L, HC))
    rows_sum.forward()
    rows_sum.wait()
    pre = npre[...] + mm(wide(ni, (1,)), wnh_all[L:])
    sig = jax.nn.sigmoid(pre)
    node_hidden = (pre * sig).astype(BF)
    node_back = (pulled * (sig * (1.0 + pre * (1.0 - sig)))).astype(BF)
    chan_n1 = ToChan(mm_nt(node_back, wnh_all[L:]), pb_n.at[1], rx_n.at[1], ch_n.at[1])
    chan_n0 = ToChan(mm_nt(node_back, wnh_all[:L]), pb_n.at[0], rx_n.at[0], ch_n.at[0])
    chan_n1.forward()
    chan_n0.forward()

    def weight_grad(g, values, back):
        per_y = g.shape[1] * g.shape[2]
        for yy in range(NY):
            part = mm_tn(values[:, yy * per_y:(yy + 1) * per_y], back)
            g[yy] = part.astype(BF).reshape(g.shape[1:])

    sc_eh, sc_eo = Scatter(g_eh, rs_bufs[0:13], True), Scatter(g_eo, rs_bufs[13:21])
    sc_nh, sc_no = Scatter(g_nh, rs_bufs[21:29]), Scatter(g_no, rs_bufs[29:37])
    weight_grad(g_nh, jnp.concatenate([wide(ni, (0,)), wide(ni, (1,))], axis=1), node_back)
    settled = len(pending)
    sc_nh.step1()
    weight_grad(g_no, cots, node_hidden)
    sc_no.step1()
    sc_nh.step1b()
    sc_no.step1b()

    chan_n1.wait()
    share = ch_n[1].reshape(N, LANE)
    get_ect.wait()
    rows_mg = ToRows(lambda g: mg.at[g])
    for j in [*far_first, 0]:
        xx = at_x(j)
        here = pl.ds(xx * RE, RE)
        total = ect[here, :].astype(F32) + mm(select_lanes(dst_b[here, :], N), share)
        ge[here, :] = total
        mgc[xx] = total.astype(BF)
        rows_mg.send(j, mgc.at[xx])
    pre = hpre[...]
    sig = jax.nn.sigmoid(pre)
    hpre[...] = sig * (1.0 + pre * (1.0 - sig))
    rows_mg.forward()
    sc_nh.step1c()
    sc_no.step1c()
    rows_mg.wait()
    message_grad = wide(mg)
    edge_back = (mm(message_grad, weo_all) * hpre[...]).astype(BF)
    def pull(t):
        return ToChan(
            mm_nt(edge_back, weh_all[t * L:(t + 1) * L]), pb_e.at[t], rx_e.at[t], ch_e.at[t]
        )

    chan_e = [pull(0)]
    weight_grad(
        g_eh, jnp.concatenate([wide(ei, (t,)) for t in range(3)], axis=1), edge_back
    )
    sc_eh.step1()
    chan_e[0].forward()
    sc_eh.step1b()
    chan_e += [pull(1), pull(2)]
    chan_e[1].forward()
    weight_grad(g_eo, message_grad, hidden[...])
    sc_eo.step1()
    chan_e[2].forward()
    sc_eo.step1b()
    sc_eh.x_step1()
    flush(settled)
    sc_nh.step2()
    sc_no.step2()

    chan_e[0].wait()
    from_source = ch_e[0].reshape(E, LANE)
    back = mm(pt[...], from_source).astype(BF)
    for p in range(NN):
        ret_out[p] = back[p * PER:(p + 1) * PER]
    returned = [
        rcopy(ret_out.at[(n + j) % NN], ret_in.at[n], n_peer(j)) for j in range(1, NN)
    ]
    ret_in[n] = ret_out[n]
    sc_eh.step1c()
    sc_eo.step1c()
    sc_nh.step3()
    sc_no.step3()
    chan_n0.wait()
    chan_e[1].wait()
    gl[...] = (
        nct[...].astype(F32)
        + ch_n[0].reshape(N, LANE).astype(F32)
        + mm(slt[...], from_source)
        + mm(dt[...], ch_e[1].reshape(E, LANE))
    )
    chan_e[2].wait()
    ge[...] = ge[...] + ch_e[2].reshape(E, LANE).astype(F32)
    put_ge = local(ge, ge_hbm, 8)
    for copy in returned:
        copy.wait_recv()
    gl[...] = gl[...] + mm_tn(
        rsel[...].reshape(NN * PER, N), ret_in[...].reshape(NN * PER, LANE)
    )
    put_gl = local(gl, gl_hbm, 9)
    out_nh[...] = node_scale * sc_nh.finish()
    out_no[...] = node_scale * sc_no.finish()
    sc_eh.step2()
    sc_eo.step2()
    sc_eh.x_step2()
    sc_eh.step3()
    sc_eo.step3()
    sc_eh.x_step3()
    out_eh[:sc_eh.main, :] = edge_scale * sc_eh.finish()
    out_eo[...] = edge_scale * sc_eo.finish()
    out_eh[sc_eh.main:, :] = edge_scale * sc_eh.x_finish()
    put_ge.wait()
    put_gl.wait()
    flush(len(pending))


def hand_over(*refs):
    count = (len(refs) - 2) // 3
    given, taken, held = refs[:count], refs[count:2 * count], refs[2 * count:3 * count]
    in_sem, out_sem = refs[3 * count:]
    loads = [
        pltpu.make_async_copy(a, b, in_sem.at[i]) for i, (a, b) in enumerate(zip(given, held))
    ]
    stores = [
        pltpu.make_async_copy(a, b, out_sem.at[i]) for i, (a, b) in enumerate(zip(held, taken))
    ]
    for load in loads:
        load.start()
    for load, store in zip(loads, stores):
        load.wait()
        store.start()
    for store in stores:
        store.wait()


def on_device(
    dims,
    latents, edge_attr, edge_src, edge_dst, send_blocks,
    edge_hidden_w, edge_out_w, node_hidden_w, node_out_w,
    node_cotangent, edge_cotangent,
):
    NX, NY, NZ = dims
    NN = NY * NZ
    E, N = edge_attr.shape[0], latents.shape[0]
    RE, RN = E // NX, N // NX
    G = NX * NC
    L, HC = G * LANE, NX * LANE
    PER = E // 2 // NN

    def v(*shape, dtype=BF):
        return pltpu.VMEM(shape, dtype)

    chunks = [3 * L // NN, 2 * L // NN, L // NN, L // NN]
    rs = []
    for i in (0, 3, 1, 2):
        part = max(16, chunks[i] // 6 // 16 * 16) if i == 0 else 0
        ch = chunks[i] - part
        rs += [
            v(NZ - 1, NY, ch, HC // 2), v(NY - 1, NZ, ch, HC // 2),
            v(NY, ch, HC // 2), v(NZ, ch, HC // 2),
            v(NY - 1, ch, HC // 2), v(NZ - 1, ch, HC // 2),
            v(ch, HC), v(NX - 1, ch, LANE),
        ]
        if part:
            rs += [
                v(NX - 1, NY, NZ, part, LANE), v(NY, NZ, part, LANE),
                v(NZ - 1, NY, part, LANE), v(NY, part, LANE), v(NY - 1, part, LANE),
            ]
    scratch = [
        pltpu.SemaphoreType.DMA((320,)), pltpu.SemaphoreType.DMA((320,)),
        pltpu.SemaphoreType.DMA((10,)),
        v(N, LANE), v(E, LANE), v(LANE, L), v(LANE, L), v(N, LANE), v(E, LANE),
        v(N, LANE, dtype=F32), v(E, LANE, dtype=F32),
        v(3, G, RE, LANE), v(2, G, RN, LANE), v(G, RN, LANE), v(G, RE, LANE),
        v(RE, HC), v(RE, HC, dtype=F32), v(RN, HC, dtype=F32),
        v(E, LANE, dtype=F32), v(E, LANE, dtype=F32), v(E, LANE, dtype=F32),
        v(N, E), v(N, E), v(NN * PER, E), v(NN, PER, N),
        *[v(NN, PER, LANE) for _ in range(6)],
        v(NX, RE, LANE), v(NX, RE, LANE), v(NX, RN, LANE), v(NX, RE, LANE),
        *[v(NY, NZ, ch, HC) for ch in chunks],
        *[v(NY, NZ, ch, HC) for ch in chunks],
        v(NX, NC, RE, LANE), v(NX, RE, LANE), v(NX, RE, LANE),
        v(2, NX, NC, RN, LANE), v(2, NX, RN, LANE), v(2, NX, RN, LANE),
        v(3, NX, NC, RE, LANE), v(3, NX, RE, LANE), v(3, NX, RE, LANE),
        *rs,
    ]
    vmem = pl.BlockSpec(memory_space=pltpu.VMEM)
    smem = pl.BlockSpec(memory_space=pltpu.SMEM)
    hbm = pl.BlockSpec(memory_space=pl.ANY)

    def f(*shape):
        return jax.ShapeDtypeStruct(shape, F32)

    results = pl.pallas_call(
        functools.partial(kernel, dims),
        out_shape=(
            f(N, LANE), f(E, LANE), f(chunks[0], LANE), f(chunks[3], LANE),
            f(chunks[1], LANE), f(chunks[2], LANE),
        ),
        in_specs=[hbm, hbm, vmem, vmem, smem] + [hbm] * 6,
        out_specs=[hbm, hbm] + [vmem] * 4,
        scratch_shapes=scratch,
        compiler_params=pltpu.CompilerParams(
            collective_id=0, has_side_effects=True, vmem_limit_bytes=64 * 1024 * 1024 - 65536
        ),
    )(
        latents, edge_attr, edge_src, edge_dst, send_blocks[0].T,
        edge_hidden_w.reshape(NY, NZ, chunks[0], LANE), edge_out_w,
        node_hidden_w.reshape(NY, NZ, chunks[1], LANE), node_out_w,
        node_cotangent, edge_cotangent,
    )
    gl, ge, g_eh, g_eo, g_nh, g_no = pl.pallas_call(
        hand_over,
        out_shape=tuple(jax.ShapeDtypeStruct(r.shape, r.dtype) for r in results),
        in_specs=[hbm] * 6,
        out_specs=[hbm] * 6,
        scratch_shapes=[
            *[pltpu.VMEM(r.shape, r.dtype) for r in results],
            pltpu.SemaphoreType.DMA((6,)), pltpu.SemaphoreType.DMA((6,)),
        ],
        compiler_params=pltpu.CompilerParams(vmem_limit_bytes=60 * 1024 * 1024),
    )(*results)
    return gl, ge, g_eh, g_eo.T, g_nh, g_no.T


def solution(mesh):
    nodes, chans = mesh.shape["node"], mesh.shape["chan"]
    nz = 1
    while nz * nz < nodes:
        nz *= 2
    dims = (chans // NC, nodes // nz, nz)
    return jax.shard_map(
        functools.partial(on_device, dims),
        mesh=mesh,
        in_specs=(
            P("node", "chan"),
            P("node", "chan"),
            P("node"),
            P("node"),
            P("node", None, None),
            P(None, "chan"),
            P("chan", None),
            P(None, "chan"),
            P("chan", None),
            P("node", "chan"),
            P("node", "chan"),
        ),
        out_specs=(
            P("node", "chan"),
            P("node", "chan"),
            P("node", "chan"),
            P("chan", "node"),
            P("node", "chan"),
            P("chan", "node"),
        ),
        check_vma=False,
    )
```
